512 devices in a mesh: dp: 32 (over z_lo, x), tensor: 16 (over y, z_hi, core).
Axes of the slice: x: 4, y: 4, z: 16 (z_hi: 2, z_lo: 8; z = z_hi * 8 + z_lo), core: 2. Of those that a mesh axis runs over, the one named last changes fastest.
Arguments:
- gate_pre: bfloat16 [4096, 14336], P('dp', 'tensor'), may hold values from -6 to 6
- up_pre: bfloat16 [4096, 14336], P('dp', 'tensor'), may hold values from -6 to 6
- weight: bfloat16 [14336, 8192], P('tensor', 'dp'), may hold values from -0.046875 to 0.046875
- basis: bfloat16 [8192, 512], P('dp'), may hold values from -0.0625 to 0.0625
- cotangent: bfloat16 [4096, 8192], P(('dp', 'tensor')), may hold values from -6 to 6
- moment1: float32 [14336, 512], P(('tensor', 'dp')), may hold values from -6 to 6
- moment2: float32 [14336, 512], P(('tensor', 'dp')), may hold values from 0.05 to 2
Outputs:
- layer_out: bfloat16 [4096, 8192], P(('dp', 'tensor'))
- grad_gate: bfloat16 [4096, 14336], P('dp', 'tensor')
- grad_up: bfloat16 [4096, 14336], P('dp', 'tensor')
- moment1_new: float32 [14336, 512], P(('tensor', 'dp'))
- moment2_new: float32 [14336, 512], P(('tensor', 'dp'))
- expansion: float32 [14336, 8192], P('tensor', 'dp')
The draws below stay inside these ranges and needn't reach their ends.
All inputs are finite; a program needn't handle non-finite values.
Results may differ from the reference program's by a relative error of at most 0.034.
Values may be sent and summed in bfloat16 or wider, within the bound.
No kernel may reach another device: no remote copies, remote signals or barrier semaphores. Data moves between devices by JAX's collectives and lax.ppermute only.
A program may use at most 128 MiB of HBM per device.

```python
import math
import jax
import jax.numpy as jnp
from jax import lax

D = 8192
FF = 14336
RANK = 512
TOKENS = 4096
N_TENSOR = 16


def level_of(rng, shape, cuts, low, high):
    gain, own = 1.0, jax.random.fold_in(rng, 6)
    for axis_at, parts in cuts:
        draws = jnp.exp(jax.random.uniform(jax.random.fold_in(own, axis_at), (parts,), jnp.float32, low / len(cuts), high / len(cuts)))
        gain = gain * jnp.repeat(draws, shape[axis_at] // parts).reshape([-1 if axis == axis_at else 1 for axis in range(len(shape))])
    return gain


def centred(own_key, extent, scale, limit, shards=(), dtype=jnp.bfloat16):
    entries = scale * jax.random.normal(own_key, extent, jnp.float32)
    if shards:
        entries = entries * level_of(own_key, extent, shards, -0.22, 0.18)
    return jnp.clip(entries, -limit, limit).astype(dtype)


def setup_inputs(seed: int = 0) -> dict:
    key_of = jax.random.split(jax.random.key(seed), 8)
    return {
        "gate_pre": centred(key_of[0], (TOKENS, FF), 1.0, 6.0, ((0, 32), (1, 16))),
        "up_pre": centred(key_of[1], (TOKENS, FF), 1.0, 6.0, ((0, 32), (1, 16))),
        "weight": centred(key_of[2], (FF, D), FF ** -0.5, 0.046875, ((0, 16), (1, 32))),
        "basis": centred(key_of[3], (D, RANK), D ** -0.5, 0.0625, ((0, 32),)),
        "cotangent": centred(key_of[4], (TOKENS, D), 1.0, 6.0, ((0, 512),)),
        "moment1": centred(key_of[5], (FF, RANK), 1.0, 6.0, ((0, 512),), jnp.float32),
        "moment2": jnp.clip(jnp.exp(math.log(2.0) - 3.6888794 * jax.random.uniform(key_of[6], (FF, RANK), jnp.float32) ** level_of(key_of[6], (FF, RANK), ((0, 512),), -0.2, 0.2)), 0.05, 2.0),
    }


corr_first = 1.0 - 0.9 ** 10
corr_second = 1.0 - 0.999 ** 10

def reference(gate_pre, up_pre, weight, basis, cotangent, moment1, moment2):
    gate_float = gate_pre.astype(jnp.float32)
    up_float = up_pre.astype(jnp.float32)
    sigmoid_gate = jax.nn.sigmoid(gate_float)
    hidden = (gate_float * sigmoid_gate * up_float).astype(jnp.bfloat16)
    block = FF // N_TENSOR
    hidden_blocks = hidden.reshape(TOKENS, N_TENSOR, block).transpose(1, 0, 2)
    weight_blocks = weight.reshape(N_TENSOR, block, D)

    def add_block(total, pieces):
        product = jnp.dot(pieces[0], pieces[1], preferred_element_type=jnp.float32)
        rounded = lax.optimization_barrier(product.astype(jnp.bfloat16))
        return (total + rounded.astype(jnp.float32), None)
    summed, _ = lax.scan(add_block, jnp.zeros((TOKENS, D), jnp.float32), (hidden_blocks, weight_blocks))
    layer_out = summed.astype(jnp.bfloat16)
    grad_hidden = lax.dot_general(cotangent, weight, (((1,), (1,)), ((), ())), preferred_element_type=jnp.float32)
    grad_up = (grad_hidden * gate_float * sigmoid_gate).astype(jnp.bfloat16)
    grad_gate = (grad_hidden * up_float * sigmoid_gate * (1.0 + gate_float * (1.0 - sigmoid_gate))).astype(jnp.bfloat16)
    reduced = jnp.dot(cotangent, basis, preferred_element_type=jnp.float32).astype(jnp.bfloat16)
    projected = lax.dot_general(hidden, reduced, (((0,), (0,)), ((), ())), preferred_element_type=jnp.float32)
    moment1_new = 0.9 * moment1 + 0.1 * projected
    moment2_new = 0.999 * moment2 + 0.001 * projected * projected
    step = (moment1_new / corr_first / (jnp.sqrt(moment2_new / corr_second) + 1e-08)).astype(jnp.bfloat16)
    expansion = lax.dot_general(step, basis, (((1,), (1,)), ((), ())), preferred_element_type=jnp.float32)
    return (layer_out, grad_gate, grad_up, moment1_new, moment2_new, expansion)
```

```python
import jax
import jax.numpy as jnp
from jax import lax
from jax.sharding import Mesh, PartitionSpec as P

corr_first = 1.0 - 0.9**10
corr_second = 1.0 - 0.999**10

NZ, NX, NY, NH, NC = 8, 4, 4, 2, 2
ORDER = (0, 2, 4, 6, 7, 5, 3, 1)
PLACE = tuple(ORDER.index(i) for i in range(NZ))
RING = [(ORDER[i], ORDER[(i + 1) % NZ]) for i in range(NZ)]
bf16, f32 = jnp.bfloat16, jnp.float32


def shift(value, axis, size, by):
    return lax.ppermute(value, axis, [(i, (i + by) % size) for i in range(size)])


def dot(a, b, contract):
    return lax.dot_general(a, b, (contract, ((), ())), preferred_element_type=f32)


def gather_ring(value, axis, size):
    index = lax.axis_index(axis)
    parts = jnp.zeros((size,) + value.shape, value.dtype)
    parts = lax.dynamic_update_index_in_dim(parts, value, index, 0)
    for by in range(1, size):
        arrived = shift(value, axis, size, by)
        parts = lax.dynamic_update_index_in_dim(parts, arrived, (index - by) % size, 0)
    return parts


def scatter_sum(parts, axis, size):
    index = lax.axis_index(axis)
    total = lax.dynamic_index_in_dim(parts, index, 0, keepdims=False).astype(f32)
    for by in range(1, size):
        piece = lax.dynamic_index_in_dim(parts, (index + by) % size, 0, keepdims=False)
        total = total + shift(piece, axis, size, by).astype(f32)
    return total


def body(gate_pre, up_pre, weight, basis, cotangent, moment1, moment2):
    zl = lax.axis_index("zl")
    order = jnp.asarray(ORDER, jnp.int32)
    place = jnp.asarray(PLACE, jnp.int32)[zl]

    gate = gate_pre.astype(f32)
    up = up_pre.astype(f32)
    sig = jax.nn.sigmoid(gate)
    hidden = (gate * sig * up).astype(bf16)
    rows, ff = hidden.shape
    mine, width = cotangent.shape
    cols = width // NZ
    rank = basis.shape[1]

    parts = cotangent.reshape(mine, NZ, cols).transpose(1, 0, 2)
    parts = jnp.broadcast_to(parts[:, None], (NZ, NH, mine, cols)).reshape(NZ * NH, mine, cols)
    got = lax.all_to_all(parts, ("zl", "zh"), 0, 0, tiled=True)
    got = gather_ring(got, "y", NY)
    other = shift(got, "c", NC, 1)
    low = lax.axis_index("c") == 0
    pair = jnp.stack([jnp.where(low, got, other), jnp.where(low, other, got)])
    cot = pair.reshape(NC, NY, NZ, NH, mine, cols).transpose(2, 1, 3, 0, 4, 5)
    cot = cot.reshape(NZ * rows, cols)

    weight_tile = gather_ring(weight, "x", NX)
    weight_tile = weight_tile.transpose(1, 0, 2).reshape(ff, cols)
    basis_tile = gather_ring(basis, "x", NX).reshape(cols, rank)

    tile = jnp.zeros((NZ, rows, ff), bf16)
    tile = lax.dynamic_update_index_in_dim(tile, hidden, zl, 0)
    moving = hidden
    for hop in range(1, NZ):
        moving = lax.ppermute(moving, "zl", RING)
        tile = lax.dynamic_update_index_in_dim(tile, moving, order[(place - hop) % NZ], 0)
    tile = tile.reshape(NZ * rows, ff)

    reduced = dot(cot, basis_tile, ((1,), (0,))).astype(bf16)
    projected = dot(tile, reduced, ((0,), (0,))).astype(bf16)
    own = moment1.shape[0]
    projected = projected.reshape(NZ, NX, own, rank).transpose(1, 0, 2, 3)
    projected = scatter_sum(projected, "x", NX).astype(bf16)
    projected = lax.all_to_all(projected, "zl", 0, 0, tiled=True).astype(f32).sum(0)
    moment1_new = 0.9 * moment1 + 0.1 * projected
    moment2_new = 0.999 * moment2 + 0.001 * projected * projected
    step = (moment1_new / corr_first / (jnp.sqrt(moment2_new / corr_second) + 1e-08)).astype(bf16)
    steps = lax.all_to_all(
        jnp.broadcast_to(step[None], (NZ, own, rank)), "zl", 0, 0, tiled=True
    )
    steps = gather_ring(steps, "x", NX).transpose(1, 0, 2, 3).reshape(ff, rank)
    expansion = dot(steps, basis, ((1,), (1,)))

    partial = dot(cot, weight_tile, ((1,), (1,))).reshape(NZ, rows, ff)
    sums = []
    half = rows // 2
    for part in range(2):
        lines = partial[:, part * half : (part + 1) * half]
        total = lax.dynamic_index_in_dim(lines, order[(place - 1) % NZ], 0, keepdims=False)
        for hop in range(NZ - 1):
            arrived = lax.ppermute(total.astype(bf16), "zl", RING)
            total = arrived.astype(f32) + lax.dynamic_index_in_dim(
                lines, order[(place - 2 - hop) % NZ], 0, keepdims=False
            )
        sums.append(total)
    grad_hidden = jnp.concatenate(sums, 0)
    grad_up = (grad_hidden * gate * sig).astype(bf16)
    grad_gate = (grad_hidden * up * sig * (1.0 + gate * (1.0 - sig))).astype(bf16)

    term = dot(tile, weight_tile, ((1,), (0,))).astype(bf16)
    term = term.reshape(NZ, NY, NH, NC, mine, cols).transpose(3, 1, 0, 2, 4, 5)
    term = scatter_sum(term, "c", NC).astype(bf16)
    term = scatter_sum(term, "y", NY).astype(bf16)
    term = lax.all_to_all(term.reshape(NZ * NH, mine, cols), ("zl", "zh"), 0, 0, tiled=True)
    term = term.reshape(NZ, NH, mine, cols).astype(f32).sum(1).astype(bf16)
    layer_out = term.transpose(1, 0, 2).reshape(mine, width)
    return (layer_out, grad_gate, grad_up, moment1_new, moment2_new, expansion)


def solution(mesh):
    fine = Mesh(mesh.devices.reshape(NZ, NX, NY, NH, NC), ("zl", "x", "y", "zh", "c"))
    dp, tensor = ("zl", "x"), ("y", "zh", "c")
    placed = (
        P(dp, tensor),
        P(dp, tensor),
        P(tensor, dp),
        P(dp, None),
        P(dp + tensor, None),
        P(tensor + dp, None),
        P(tensor + dp, None),
    )
    return jax.shard_map(
        body,
        mesh=fine,
        in_specs=placed,
        out_specs=(
            P(dp + tensor, None),
            P(dp, tensor),
            P(dp, tensor),
            P(tensor + dp, None),
            P(tensor + dp, None),
            P(tensor, dp),
        ),
        check_vma=False,
    )
```

```python
import jax
import jax.numpy as jnp
from jax import lax
from jax.experimental import pallas as pl
from jax.experimental.pallas import tpu as pltpu
from jax.sharding import Mesh, PartitionSpec as P

corr_first = 1.0 - 0.9**10
corr_second = 1.0 - 0.999**10

NZ, NX, NY, NH, NC = 8, 4, 4, 2, 2
bf16, f32 = jnp.bfloat16, jnp.float32
VMEM = pl.BlockSpec(memory_space=pltpu.VMEM)
SMEM = pl.BlockSpec(memory_space=pltpu.SMEM)


def shift(value, axis, size, by):
    return lax.ppermute(value, axis, [(i, (i - by) % size) for i in range(size)])


def dot(a, b, contract):
    return lax.dot_general(a, b, (contract, ((), ())), preferred_element_type=f32)


def call(kernel, n_in, outs, scratch=(), flops=0, limit=32):
    return pl.pallas_call(
        kernel,
        out_shape=tuple(jax.ShapeDtypeStruct(*o) for o in outs),
        in_specs=[SMEM] + [VMEM] * n_in,
        out_specs=tuple(VMEM for _ in outs),
        scratch_shapes=[pltpu.VMEM(*s) for s in scratch],
        compiler_params=pltpu.CompilerParams(vmem_limit_bytes=limit << 20),
        cost_estimate=pl.CostEstimate(flops=flops, bytes_accessed=4 << 20, transcendentals=0),
    )


def prepare(pos, gate, up, cot, hidden, pack, natural):
    x, y, c = pos[0], pos[1], pos[2]
    g = gate[...].astype(f32)
    natural[...] = g * jax.nn.sigmoid(g) * up[...].astype(f32)
    for cr in range(NC):
        for yr in range(NY):
            first = (lax.rem(y + yr, NY) * 4 + lax.rem(c + cr, NC)) * 8
            pair = [natural[pl.ds(pl.multiple_of(first + zh * 16, 8), 8), :] for zh in range(NH)]
            hidden[pl.ds((cr * NY + yr) * 16, 16), :] = jnp.concatenate(pair, 0).astype(bf16)
    for r in range(NX):
        block = lax.rem(x + r, NX) * 256
        for zl in range(NZ):
            piece = cot[:, pl.ds(pl.multiple_of(zl * 1024 + block, 256), 256)]
            for zh in range(NH):
                pack[zl * NH + zh, :, r * 256 : (r + 1) * 256] = piece


def backward(pos, *refs):
    cots, weights, bases = refs[:8], refs[8:12], refs[12:16]
    grad, reduced, tile = refs[16:]
    for piece in range(8):
        for zl in range(NZ):
            tile[pl.ds(zl * 128 + piece * 16, 16), :] = cots[piece][pl.ds(zl * 16, 16), :]

    def rows(step, _):
        at = pl.ds(pl.multiple_of(step * 256, 256), 256)
        total, low = None, None
        for r in range(NX):
            part = tile[at, r * 256 : (r + 1) * 256]
            more = dot(part, weights[r][...], ((1,), (1,)))
            total = more if total is None else total + more
            more = dot(part, bases[r][...], ((1,), (0,)))
            low = more if low is None else low + more
        grad[at, :] = total.astype(bf16)
        reduced[at, :] = low.astype(bf16)
        return 0

    lax.fori_loop(0, 4, rows, 0)


def project(pos, tile, reduced, out, total):
    x = pos[0]
    total[...] = dot(tile[...], reduced[...], ((0,), (0,)))
    for xs in range(NX):
        to = lax.rem(xs - x + NX, NX)
        for zl in range(NZ):
            out[to, zl, :, :] = total[zl * 112 + xs * 28 : zl * 112 + xs * 28 + 28, :].astype(bf16)


def forward(pos, tile, w0, w1, w2, w3, out):
    def rows(step, _):
        at = pl.ds(pl.multiple_of(step * 256, 256), 256)
        part = tile[at, :]
        for r, w in enumerate((w0, w1, w2, w3)):
            term = dot(part, w[...], ((1,), (0,))).astype(bf16)
            for half in range(2):
                for piece in range(8):
                    first = half * 128 + piece * 16
                    to = pl.ds(pl.multiple_of((step * 2 + half) * 16, 16), 16)
                    out[piece // 4, piece % 4, to, r * 256 : (r + 1) * 256] = term[first : first + 16, :]
        return 0

    lax.fori_loop(0, 4, rows, 0)


def finish_out(pos, parts, out):
    x = pos[0]
    for zl in range(NZ):
        both = (parts[zl * NH].astype(f32) + parts[zl * NH + 1].astype(f32)).astype(bf16)
        for r in range(NX):
            block = zl * 1024 + lax.rem(x + r, NX) * 256
            out[:, pl.ds(pl.multiple_of(block, 256), 256)] = both[:, r * 256 : (r + 1) * 256]


def finish_grad(pos, total, gate, up, grad_gate, grad_up, relative, natural):
    y, c = pos[1], pos[2]
    relative[...] = total[...].astype(f32)
    for ys in range(NY):
        yr = lax.rem(ys - y + NY, NY)
        for zh in range(NH):
            for cs in range(NC):
                cr = lax.rem(cs + c, NC)
                first = ((cr * NY + yr) * NH + zh) * 8
                natural[((ys * NH + zh) * NC + cs) * 8 : ((ys * NH + zh) * NC + cs) * 8 + 8, :] = (
                    relative[pl.ds(pl.multiple_of(first, 8), 8), :]
                )
    g, u, d = gate[...].astype(f32), up[...].astype(f32), natural[...]
    s = jax.nn.sigmoid(g)
    grad_up[...] = (d * g * s).astype(bf16)
    grad_gate[...] = (d * u * s * (1.0 + g * (1.0 - s))).astype(bf16)


def expand(pos, s0, s1, s2, s3, basis, out, pieces, steps):
    x = pos[0]
    for r, piece in enumerate((s0, s1, s2, s3)):
        pieces[lax.rem(x + r, NX)] = piece[...].astype(f32)
    for xs in range(NX):
        for zl in range(NZ):
            steps[zl * 112 + xs * 28 : zl * 112 + xs * 28 + 28, :] = pieces[xs, zl]
    out[...] = dot(steps[...].astype(bf16), basis[...], ((1,), (1,)))


def body(gate, up, weight, basis, cotangent, moment1, moment2):
    pos = jnp.stack([lax.axis_index(a).astype(jnp.int32) for a in ("x", "y", "c")])
    rows, ff = gate.shape
    mine, width = cotangent.shape
    cols = width // NZ
    rank = basis.shape[1]
    own = moment1.shape[0]

    hidden, pack = call(
        prepare, 3, [((rows, ff), bf16), ((NZ * NH, mine, cols), bf16)], [((rows, ff), f32)]
    )(pos, gate, up, cotangent)
    tile = lax.all_gather(hidden, "zl", axis=0, tiled=True)

    got = lax.all_to_all(pack, ("zl", "zh"), 0, 0, tiled=True).reshape(rows, cols)
    cots = [got] + [shift(got, "y", NY, by) for by in range(1, NY)]
    cots = cots + [shift(piece, "c", NC, 1) for piece in cots]
    bases = [basis] + [shift(basis, "x", NX, by) for by in range(1, NX)]
    weights = [weight] + [shift(weight, "x", NX, by) for by in range(1, NX)]

    partial, reduced = call(
        backward,
        16,
        [((NZ * rows, ff), bf16), ((NZ * rows, rank), bf16)],
        [((NZ * rows, cols), bf16)],
        flops=3 * 10**9,
    )(pos, *cots, *weights, *bases)
    grad_hidden = lax.psum_scatter(partial, "zl", scatter_dimension=0, tiled=True)
    grad_gate, grad_up = call(
        finish_grad,
        3,
        [((rows, ff), bf16), ((rows, ff), bf16)],
        [((rows, ff), f32), ((rows, ff), f32)],
    )(pos, grad_hidden, gate, up)

    (parts,) = call(
        project, 2, [((NX, NZ, own, rank), bf16)], [((ff, rank), f32)], flops=10**9
    )(pos, tile, reduced)
    projected = parts[0].astype(f32)
    for by in range(1, NX):
        projected = projected + shift(parts[by], "x", NX, -by).astype(f32)
    projected = lax.all_to_all(projected.astype(bf16), "zl", 0, 0, tiled=True).astype(f32).sum(0)
    moment1_new = 0.9 * moment1 + 0.1 * projected
    moment2_new = 0.999 * moment2 + 0.001 * projected * projected
    step = (moment1_new / corr_first / (jnp.sqrt(moment2_new / corr_second) + 1e-08)).astype(bf16)
    steps = lax.all_to_all(
        jnp.broadcast_to(step[None], (NZ, own, rank)), "zl", 0, 0, tiled=True
    )
    steps = [steps] + [shift(steps, "x", NX, by) for by in range(1, NX)]
    (expansion,) = call(
        expand,
        5,
        [((ff, basis.shape[0]), f32)],
        [((NX, NZ, own, rank), f32), ((ff, rank), f32)],
        flops=3 * 10**8,
    )(pos, *steps, basis)

    (term,) = call(forward, 5, [((NC, NY, rows, cols), bf16)], flops=2 * 10**9)(
        pos, tile, *weights
    )
    term = (term[0].astype(f32) + shift(term[1], "c", NC, 1).astype(f32)).astype(bf16)
    total = term[0].astype(f32)
    for by in range(1, NY):
        total = total + shift(term[by], "y", NY, -by).astype(f32)
    total = total.astype(bf16).reshape(NZ * NH, mine, cols)
    total = lax.all_to_all(total, ("zl", "zh"), 0, 0, tiled=True)
    (layer_out,) = call(finish_out, 1, [((mine, width), bf16)])(pos, total)
    return (layer_out, grad_gate, grad_up, moment1_new, moment2_new, expansion)


def solution(mesh):
    fine = Mesh(mesh.devices.reshape(NZ, NX, NY, NH, NC), ("zl", "x", "y", "zh", "c"))
    dp, tensor = ("zl", "x"), ("y", "zh", "c")
    placed = (
        P(dp, tensor),
        P(dp, tensor),
        P(tensor, dp),
        P(dp, None),
        P(dp + tensor, None),
        P(tensor + dp, None),
        P(tensor + dp, None),
    )
    return jax.shard_map(
        body,
        mesh=fine,
        in_specs=placed,
        out_specs=(
            P(dp + tensor, None),
            P(dp, tensor),
            P(dp, tensor),
            P(tensor + dp, None),
            P(tensor + dp, None),
            P(tensor, dp),
        ),
        check_vma=False,
    )
```

```python
import jax
import jax.numpy as jnp
from jax import lax
from jax.experimental import pallas as pl
from jax.experimental.pallas import tpu as pltpu
from jax.sharding import Mesh, PartitionSpec as P

corr_first = 1.0 - 0.9**10
corr_second = 1.0 - 0.999**10

NA, NB, NX, NY, NH, NC = 2, 4, 4, 4, 2, 2
NZ = NA * NB
bf16, f32 = jnp.bfloat16, jnp.float32
VMEM = pl.BlockSpec(memory_space=pltpu.VMEM)
SMEM = pl.BlockSpec(memory_space=pltpu.SMEM)


def spread(value, axes, size):
    copies = jnp.broadcast_to(value[None], (size,) + value.shape)
    return lax.all_to_all(copies, axes, 0, 0, tiled=True)


def swap(value, axis):
    return lax.ppermute(value, axis, [(0, 1), (1, 0)])


def dot(a, b, contract):
    return lax.dot_general(a, b, (contract, ((), ())), preferred_element_type=f32)


def call(kernel, n_in, outs, scratch=(), flops=0, limit=32):
    return pl.pallas_call(
        kernel,
        out_shape=tuple(jax.ShapeDtypeStruct(*o) for o in outs),
        in_specs=[SMEM] + [VMEM] * n_in,
        out_specs=tuple(VMEM for _ in outs),
        scratch_shapes=[pltpu.VMEM(*s) for s in scratch],
        compiler_params=pltpu.CompilerParams(vmem_limit_bytes=limit << 20),
        cost_estimate=pl.CostEstimate(flops=flops, bytes_accessed=4 << 20, transcendentals=0),
    )


def prepare(pos, gate, up, cot, hidden, pack, plain):
    c = pos[1]
    g = gate[...].astype(f32)
    plain[...] = g * jax.nn.sigmoid(g) * up[...].astype(f32)
    for cr in range(NC):
        for y in range(NY):
            first = (y * 4 + lax.rem(c + cr, NC)) * 8
            pair = [plain[pl.ds(pl.multiple_of(first + zh * 16, 8), 8), :] for zh in range(NH)]
            hidden[pl.ds((cr * NY + y) * 16, 16), :] = jnp.concatenate(pair, 0).astype(bf16)
    for za in range(NA):
        for x in range(NX):
            for zb in range(NB):
                block = ((za * NB + zb) * NX + x) * 256
                piece = cot[:, block : block + 256]
                for zh in range(NH):
                    pack[(za * NX + x) * NH + zh, :, zb * 256 : (zb + 1) * 256] = piece


def project(pos, cot_own, cot_other, basis_own, basis_other, hidden, tile, out, basis, reduced, total):
    za, c = pos[0], pos[1]
    for hr, part in enumerate((basis_own, basis_other)):
        for zb in range(NB):
            first = zb * 256 + lax.rem(c + hr, NC) * 128
            basis[pl.ds(pl.multiple_of(first, 128), 128), :] = part[zb]
    for x in range(NX):
        for ar in range(NA):
            at = pl.ds(pl.multiple_of((lax.rem(za + ar, NA) * NX + x) * 16, 16), 16)
            for cr, cot in enumerate((cot_own, cot_other)):
                for y in range(NY):
                    to = (x * NA + ar) * 128 + (cr * NY + y) * 16
                    tile[to : to + 16, :] = cot[y, at, :]

    def rows(step, _):
        at = pl.ds(pl.multiple_of(step * 256, 256), 256)
        reduced[at, :] = dot(tile[at, :], basis[...], ((1,), (0,))).astype(bf16)
        return 0

    lax.fori_loop(0, 4, rows, 0)
    total[...] = dot(hidden[...], reduced[...], ((0,), (0,)))
    spare = jnp.zeros((4, total.shape[1]), f32)
    for x in range(NX):
        for zl in range(NZ):
            first = zl * 112 + x * 28
            block = jnp.concatenate([total[first : first + 28, :], spare], 0)
            out[x, zl * 32 : zl * 32 + 32, :] = block.astype(bf16)


def backward(pos, tile, weight, out):
    def rows(x, _):
        at = pl.ds(pl.multiple_of(x * 256, 256), 256)
        total = None
        for zb in range(NB):
            more = dot(tile[at, zb * 256 : (zb + 1) * 256], weight[zb], ((1,), (1,)))
            total = more if total is None else total + more
        out[x] = total.astype(bf16)
        return 0

    lax.fori_loop(0, NX, rows, 0)


def forward(pos, hidden, weight, out):
    za = pos[0]

    def rows(x, _):
        part = hidden[pl.ds(pl.multiple_of(x * 256, 256), 256), :]
        for zb in range(NB):
            term = dot(part, weight[zb], ((1,), (0,))).astype(bf16)
            for ar in range(NA):
                to = (lax.rem(za + ar, NA) * NX + x) * 16
                to = pl.ds(pl.multiple_of(to, 16), 16)
                for piece in range(8):
                    first = ar * 128 + piece * 16
                    out[piece // 4, piece % 4, to, zb * 256 : (zb + 1) * 256] = term[first : first + 16, :]
        return 0

    lax.fori_loop(0, NX, rows, 0)


def finish_out(pos, parts, out):
    for za in range(NA):
        for x in range(NX):
            at = (za * NX + x) * NH
            both = (parts[at].astype(f32) + parts[at + 1].astype(f32)).astype(bf16)
            for zb in range(NB):
                block = ((za * NB + zb) * NX + x) * 256
                out[:, block : block + 256] = both[:, zb * 256 : (zb + 1) * 256]


def finish_grad(pos, parts, arrived, gate, up, grad_gate, grad_up, relative, plain):
    c = pos[1]
    total = arrived[...].astype(f32)
    for x in range(NX):
        total = total + parts[x, :128, :].astype(f32)
    relative[...] = total
    for y in range(NY):
        for zh in range(NH):
            for cs in range(NC):
                cr = lax.rem(cs + c, NC)
                first = ((cr * NY + y) * NH + zh) * 8
                to = ((y * NH + zh) * NC + cs) * 8
                plain[to : to + 8, :] = relative[pl.ds(pl.multiple_of(first, 8), 8), :]
    g, u, d = gate[...].astype(f32), up[...].astype(f32), plain[...]
    s = jax.nn.sigmoid(g)
    grad_up[...] = (d * g * s).astype(bf16)
    grad_gate[...] = (d * u * s * (1.0 + g * (1.0 - s))).astype(bf16)


def expand(pos, parts, basis, out, steps):
    for x in range(NX):
        for zl in range(NZ):
            first = zl * 112 + x * 28
            steps[first : first + 28, :] = parts[x, zl * 32 : zl * 32 + 32, :].astype(f32)[:28]
    out[...] = dot(steps[...].astype(bf16), basis[...], ((1,), (1,)))


def body(gate, up, weight, basis, cotangent, moment1, moment2):
    za, c = lax.axis_index("za"), lax.axis_index("c")
    pos = jnp.stack([za, c]).astype(jnp.int32)
    rows, ff = gate.shape
    mine, width = cotangent.shape
    deep, rank = basis.shape
    cols = NB * deep
    own, slot = moment1.shape[0], 32
    square = ("za", "x", "zh")
    line = ("za", "zb")

    hidden, pack = call(
        prepare, 3, [((rows, ff), bf16), ((NA * NX * NH, mine, cols), bf16)], [((rows, ff), f32)]
    )(pos, gate, up, cotangent)

    cot = lax.all_to_all(pack, square, 0, 0, tiled=True).reshape(rows, cols)
    half = deep // NC
    basis_part = spread(lax.dynamic_slice_in_dim(basis, c * half, half, 0), "zb", NB)
    pair = jnp.concatenate([hidden, swap(hidden, "za")], 0)
    weights = spread(weight, "zb", NB)
    cot = spread(cot, "y", NY)
    tile_hidden = spread(pair, "x", NX).reshape(NX * NA * rows, ff)

    tile, parts = call(
        project,
        5,
        [((NX * NA * rows, cols), bf16), ((NX, NZ * slot, rank), bf16)],
        [((cols, rank), bf16), ((NX * NA * rows, rank), bf16), ((ff, rank), f32)],
        flops=2 * 10**9,
    )(pos, cot, swap(cot, "c"), basis_part, swap(basis_part, "c"), tile_hidden)

    parts = lax.all_to_all(parts, "x", 0, 0, tiled=True).astype(f32).sum(0).astype(bf16)
    parts = lax.all_to_all(parts, line, 0, 0, tiled=True).reshape(NZ, slot, rank)
    projected = parts.astype(f32).sum(0)[:own]
    moment1_new = 0.9 * moment1 + 0.1 * projected
    moment2_new = 0.999 * moment2 + 0.001 * projected * projected
    step = (moment1_new / corr_first / (jnp.sqrt(moment2_new / corr_second) + 1e-08)).astype(bf16)
    step = jnp.pad(step, ((0, slot - own), (0, 0)))
    steps = spread(spread(step, line, NZ).reshape(NZ * slot, rank), "x", NX)
    (expansion,) = call(
        expand, 2, [((ff, deep), f32)], [((ff, rank), f32)], flops=3 * 10**8
    )(pos, steps, basis)

    (partial,) = call(backward, 2, [((NX, NA * rows, ff), bf16)], flops=2 * 10**9)(
        pos, tile, weights
    )
    partial = lax.all_to_all(partial, "x", 0, 0, tiled=True)
    arrived = swap(partial[:, rows:].astype(f32).sum(0).astype(bf16), "za")
    grad_gate, grad_up = call(
        finish_grad,
        4,
        [((rows, ff), bf16), ((rows, ff), bf16)],
        [((rows, ff), f32), ((rows, ff), f32)],
    )(pos, partial, arrived, gate, up)

    (term,) = call(forward, 2, [((NC, NY, rows, cols), bf16)], flops=2 * 10**9)(
        pos, tile_hidden, weights
    )
    term = (term[0].astype(f32) + swap(term[1], "c").astype(f32)).astype(bf16)
    term = lax.all_to_all(term, "y", 0, 0, tiled=True).astype(f32).sum(0).astype(bf16)
    term = lax.all_to_all(
        term.reshape(NA * NX * NH, mine, cols), square, 0, 0, tiled=True
    )
    (layer_out,) = call(finish_out, 1, [((mine, width), bf16)])(pos, term)
    return (layer_out, grad_gate, grad_up, moment1_new, moment2_new, expansion)


def solution(mesh):
    names = ("za", "zb", "x", "y", "zh", "c")
    fine = Mesh(mesh.devices.reshape(NA, NB, NX, NY, NH, NC), names)
    dp, tensor = ("za", "zb", "x"), ("y", "zh", "c")
    placed = (
        P(dp, tensor),
        P(dp, tensor),
        P(tensor, dp),
        P(dp, None),
        P(dp + tensor, None),
        P(tensor + dp, None),
        P(tensor + dp, None),
    )
    return jax.shard_map(
        body,
        mesh=fine,
        in_specs=placed,
        out_specs=(
            P(dp + tensor, None),
            P(dp, tensor),
            P(dp, tensor),
            P(tensor + dp, None),
            P(tensor + dp, None),
            P(tensor, dp),
        ),
        check_vma=False,
    )
```

```python
import jax
import jax.numpy as jnp
from jax import lax
from jax.experimental import pallas as pl
from jax.experimental.pallas import tpu as pltpu
from jax.sharding import Mesh, PartitionSpec as P

corr_first = 1.0 - 0.9**10
corr_second = 1.0 - 0.999**10

NA, NB, NX, NY, NH, NC = 2, 4, 4, 4, 2, 2
NZ = NA * NB
ORDER = (0, 1, 3, 2)
RING = [(ORDER[i], ORDER[(i + 1) % NB]) for i in range(NB)]
bf16, f32 = jnp.bfloat16, jnp.float32
VMEM = pl.BlockSpec(memory_space=pltpu.VMEM)
SMEM = pl.BlockSpec(memory_space=pltpu.SMEM)


def shift(value, axis, size, by):
    return lax.ppermute(value, axis, [(i, (i - by) % size) for i in range(size)])


def swap(value, axis):
    return lax.ppermute(value, axis, [(0, 1), (1, 0)])


def dot(a, b, contract):
    return lax.dot_general(a, b, (contract, ((), ())), preferred_element_type=f32)


def call(kernel, n_in, outs, scratch=(), flops=0, limit=32):
    return pl.pallas_call(
        kernel,
        out_shape=tuple(jax.ShapeDtypeStruct(*o) for o in outs),
        in_specs=[SMEM] + [VMEM] * n_in,
        out_specs=tuple(VMEM for _ in outs),
        scratch_shapes=[pltpu.VMEM(*s) for s in scratch],
        compiler_params=pltpu.CompilerParams(vmem_limit_bytes=limit << 20),
        cost_estimate=pl.CostEstimate(flops=flops, bytes_accessed=4 << 20, transcendentals=0),
    )


def ring_block(zb, hop):
    place = ((zb ^ (zb >> 1)) - hop) & (NB - 1)
    return place ^ (place >> 1)


def prepare(pos, gate, up, cot, weight, basis, hidden, pack, both, plain):
    y, c = pos[2], pos[3]
    for za in range(NA):
        for x in range(NX):
            for r in range(NB):
                block = ((za * NB + ring_block(pos[4], r)) * NX + x) * 256
                piece = cot[:, pl.ds(pl.multiple_of(block, 256), 256)]
                for zh in range(NH):
                    pack[(za * NX + x) * NH + zh, :, r * 256 : (r + 1) * 256] = piece
    both[:896, :] = weight[...]
    both[896:1152, :] = basis[:, :256]
    both[1152:, :] = basis[:, 256:]
    g = gate[...].astype(f32)
    plain[...] = g * jax.nn.sigmoid(g) * up[...].astype(f32)
    for cr in range(NC):
        for yr in range(NY):
            first = (lax.rem(y + yr, NY) * 4 + lax.rem(c + cr, NC)) * 8
            pair = [plain[pl.ds(pl.multiple_of(first + zh * 16, 8), 8), :] for zh in range(NH)]
            hidden[pl.ds((cr * NY + yr) * 16, 16), :] = jnp.concatenate(pair, 0).astype(bf16)


def project(pos, *refs):
    cots, boths, hiddens = refs[:8], refs[8:12], refs[12:16]
    tile, outs, reduced, total, blocks = refs[16], refs[17:21], *refs[21:]
    za, x = pos[0], pos[1]
    for xr in range(NX):
        for ar in range(NA):
            at = (lax.rem(za + ar, NA) * NX + lax.rem(x + xr, NX)) * 16
            at = pl.ds(pl.multiple_of(at, 16), 16)
            for piece in range(8):
                to = (xr * NA + ar) * 128 + piece * 16
                tile[to : to + 16, :] = cots[piece][at, :]

    def rows(step, _):
        at = pl.ds(pl.multiple_of(step * 256, 256), 256)
        for side in range(2):
            low = None
            for r in range(NB):
                part = boths[r][896 + side * 256 : 1152 + side * 256, :]
                more = dot(tile[at, r * 256 : (r + 1) * 256], part, ((1,), (0,)))
                low = more if low is None else low + more
            reduced[at, side * 256 : (side + 1) * 256] = low.astype(bf16)
        return 0

    lax.fori_loop(0, 4, rows, 0)
    for xr in range(NX):
        more = dot(hiddens[xr][...], reduced[xr * 256 : (xr + 1) * 256, :], ((0,), (0,)))
        total[...] = more if xr == 0 else total[...] + more
    spare = jnp.zeros((4, total.shape[1]), f32)
    for xs in range(NX):
        for zl in range(NZ):
            first = zl * 112 + xs * 28
            block = jnp.concatenate([total[first : first + 28, :], spare], 0)
            blocks[xs, zl * 32 : zl * 32 + 32, :] = block.astype(bf16)
    for xr, out in enumerate(outs):
        out[...] = blocks[lax.rem(x + xr, NX)]


def backward(pos, tile, b0, b1, b2, b3, *outs):
    for xr, out in enumerate(outs):
        total = None
        for r, both in enumerate((b0, b1, b2, b3)):
            part = tile[xr * 256 : (xr + 1) * 256, r * 256 : (r + 1) * 256]
            more = dot(part, both[:896, :], ((1,), (1,)))
            total = more if total is None else total + more
        out[...] = total.astype(bf16)


def forward(pos, b0, b1, b2, b3, h0, h1, h2, h3, o0, o1, o2, o3, leave):
    za, x = pos[0], pos[1]
    for xr, hidden in enumerate((h0, h1, h2, h3)):
        for r, both in enumerate((b0, b1, b2, b3)):
            term = dot(hidden[...], both[:896, :], ((1,), (0,))).astype(bf16)
            for ar in range(NA):
                to = (lax.rem(za + ar, NA) * NX + lax.rem(x + xr, NX)) * 16
                to = pl.ds(pl.multiple_of(to, 16), 16)
                for piece in range(8):
                    first = ar * 128 + piece * 16
                    block = term[first : first + 16, :]
                    if piece < NY:
                        (o0, o1, o2, o3)[piece][to, r * 256 : (r + 1) * 256] = block
                    else:
                        leave[piece - NY, to, r * 256 : (r + 1) * 256] = block


def finish_out(pos, parts, out):
    for za in range(NA):
        for x in range(NX):
            at = (za * NX + x) * NH
            pair = (parts[at].astype(f32) + parts[at + 1].astype(f32)).astype(bf16)
            for r in range(NB):
                block = ((za * NB + ring_block(pos[4], r)) * NX + x) * 256
                to = pl.ds(pl.multiple_of(block, 256), 256)
                out[:, to] = pair[:, r * 256 : (r + 1) * 256]


def finish_grad(pos, p0, p1, p2, p3, arrived, gate, up, grad_gate, grad_up, relative, plain):
    y, c = pos[2], pos[3]
    total = arrived[...].astype(f32)
    for part in (p0, p1, p2, p3):
        total = total + part[:128, :].astype(f32)
    relative[...] = total
    for ys in range(NY):
        yr = lax.rem(ys - y + NY, NY)
        for zh in range(NH):
            for cs in range(NC):
                cr = lax.rem(cs + c, NC)
                first = ((cr * NY + yr) * NH + zh) * 8
                to = ((ys * NH + zh) * NC + cs) * 8
                plain[to : to + 8, :] = relative[pl.ds(pl.multiple_of(first, 8), 8), :]
    g, u, d = gate[...].astype(f32), up[...].astype(f32), plain[...]
    s = jax.nn.sigmoid(g)
    grad_up[...] = (d * g * s).astype(bf16)
    grad_gate[...] = (d * u * s * (1.0 + g * (1.0 - s))).astype(bf16)


def expand(pos, s0, s1, s2, s3, basis, out, pieces, steps):
    x = pos[1]
    for xr, piece in enumerate((s0, s1, s2, s3)):
        pieces[lax.rem(x + xr, NX)] = piece[...].astype(f32)
    for xs in range(NX):
        for zl in range(NZ):
            first = zl * 112 + xs * 28
            steps[first : first + 28, :] = pieces[xs, zl * 32 : zl * 32 + 28, :]
    out[...] = dot(steps[...].astype(bf16), basis[...], ((1,), (1,)))


def body(gate, up, weight, basis, cotangent, moment1, moment2):
    pos = jnp.stack([lax.axis_index(a) for a in ("za", "x", "y", "c", "zb")]).astype(jnp.int32)
    rows, ff = gate.shape
    mine, width = cotangent.shape
    deep, rank = basis.shape
    cols = NB * deep
    own, slot = moment1.shape[0], 32
    square = ("za", "x", "zh")
    line = ("za", "zb")

    hidden, pack, both = call(
        prepare,
        5,
        [
            ((rows, ff), bf16),
            ((NA * NX * NH, mine, cols), bf16),
            ((ff + 2 * deep, deep), bf16),
        ],
        [((rows, ff), f32)],
    )(pos, gate, up, cotangent, weight, basis)

    cot = lax.all_to_all(pack, square, 0, 0, tiled=True).reshape(rows, cols)
    pair = jnp.concatenate([hidden, swap(hidden, "za")], 0)
    boths = [both]
    for _ in range(1, NB):
        boths.append(lax.ppermute(boths[-1], "zb", RING))
    hiddens = [pair] + [shift(pair, "x", NX, by) for by in range(1, NX)]
    cots = [cot] + [shift(cot, "y", NY, by) for by in range(1, NY)]
    cots = cots + [swap(piece, "c") for piece in cots]

    tile, *parts = call(
        project,
        16,
        [((NX * NA * rows, cols), bf16)] + [((NZ * slot, rank), bf16)] * NX,
        [((NX * NA * rows, rank), bf16), ((ff, rank), f32), ((NX, NZ * slot, rank), bf16)],
        flops=2 * 10**9,
    )(pos, *cots, *boths, *hiddens)

    total = parts[0].astype(f32)
    for by in range(1, NX):
        total = total + shift(parts[by], "x", NX, -by).astype(f32)
    total = lax.all_to_all(total.astype(bf16), line, 0, 0, tiled=True).reshape(NZ, slot, rank)
    projected = total.astype(f32).sum(0)[:own]
    moment1_new = 0.9 * moment1 + 0.1 * projected
    moment2_new = 0.999 * moment2 + 0.001 * projected * projected
    step = (moment1_new / corr_first / (jnp.sqrt(moment2_new / corr_second) + 1e-08)).astype(bf16)
    step = jnp.pad(step, ((0, slot - own), (0, 0)))
    step = jnp.broadcast_to(step[None], (NZ, slot, rank))
    step = lax.all_to_all(step, line, 0, 0, tiled=True).reshape(NZ * slot, rank)
    steps = [step] + [shift(step, "x", NX, by) for by in range(1, NX)]
    (expansion,) = call(
        expand,
        5,
        [((ff, deep), f32)],
        [((NX, NZ * slot, rank), f32), ((ff, rank), f32)],
        flops=3 * 10**8,
    )(pos, *steps, basis)

    partial = call(backward, 5, [((NA * rows, ff), bf16)] * NX, flops=2 * 10**9)(
        pos, tile, *boths
    )
    partials = [partial[0]] + [shift(partial[by], "x", NX, -by) for by in range(1, NX)]
    leave = partials[0][rows:].astype(f32)
    for part in partials[1:]:
        leave = leave + part[rows:].astype(f32)
    arrived = swap(leave.astype(bf16), "za")
    grad_gate, grad_up = call(
        finish_grad,
        7,
        [((rows, ff), bf16), ((rows, ff), bf16)],
        [((rows, ff), f32), ((rows, ff), f32)],
    )(pos, *partials, arrived, gate, up)

    *term, leave = call(
        forward, 8, [((rows, cols), bf16)] * NY + [((NY, rows, cols), bf16)], flops=2 * 10**9
    )(pos, *boths, *hiddens)
    arrived = swap(leave, "c")
    term = [(term[yr].astype(f32) + arrived[yr].astype(f32)).astype(bf16) for yr in range(NY)]
    total = term[0].astype(f32)
    for by in range(1, NY):
        total = total + shift(term[by], "y", NY, -by).astype(f32)
    total = total.astype(bf16).reshape(NA * NX * NH, mine, cols)
    total = lax.all_to_all(total, square, 0, 0, tiled=True)
    (layer_out,) = call(finish_out, 1, [((mine, width), bf16)])(pos, total)
    return (layer_out, grad_gate, grad_up, moment1_new, moment2_new, expansion)


def solution(mesh):
    names = ("za", "zb", "x", "y", "zh", "c")
    fine = Mesh(mesh.devices.reshape(NA, NB, NX, NY, NH, NC), names)
    dp, tensor = ("za", "zb", "x"), ("y", "zh", "c")
    placed = (
        P(dp, tensor),
        P(dp, tensor),
        P(tensor, dp),
        P(dp, None),
        P(dp + tensor, None),
        P(tensor + dp, None),
        P(tensor + dp, None),
    )
    return jax.shard_map(
        body,
        mesh=fine,
        in_specs=placed,
        out_specs=(
            P(dp + tensor, None),
            P(dp, tensor),
            P(dp, tensor),
            P(tensor + dp, None),
            P(tensor + dp, None),
            P(tensor, dp),
        ),
        check_vma=False,
    )
```

```python
import jax
import jax.numpy as jnp
from jax import lax
from jax.experimental import pallas as pl
from jax.experimental.pallas import tpu as pltpu
from jax.sharding import Mesh, PartitionSpec as P

corr_first = 1.0 - 0.9**10
corr_second = 1.0 - 0.999**10

NZ, NX, NY, NH, NC = 8, 4, 4, 2, 2
ORDER = (0, 2, 4, 6, 7, 5, 3, 1)
RING = [(ORDER[i], ORDER[(i + 1) % NZ]) for i in range(NZ)]
bf16, f32 = jnp.bfloat16, jnp.float32
VMEM = pl.BlockSpec(memory_space=pltpu.VMEM)
SMEM = pl.BlockSpec(memory_space=pltpu.SMEM)


def shift(value, axis, size, by):
    return lax.ppermute(value, axis, [(i, (i - by) % size) for i in range(size)])


def dot(a, b, contract):
    return lax.dot_general(a, b, (contract, ((), ())), preferred_element_type=f32)


def call(kernel, n_in, outs, scratch=(), flops=0, limit=20):
    return pl.pallas_call(
        kernel,
        out_shape=tuple(jax.ShapeDtypeStruct(*o) for o in outs),
        in_specs=[SMEM] + [VMEM] * n_in,
        out_specs=tuple(VMEM for _ in outs),
        scratch_shapes=[pltpu.VMEM(*s) for s in scratch],
        compiler_params=pltpu.CompilerParams(vmem_limit_bytes=limit << 20),
        cost_estimate=pl.CostEstimate(flops=flops, bytes_accessed=4 << 20, transcendentals=0),
    )


def ring_block(zl, hop):
    half = zl >> 1
    place = jnp.where((zl & 1) == 0, half, NZ - 1 - half)
    place = (place - hop) & (NZ - 1)
    return jnp.where(place < NZ // 2, 2 * place, 2 * NZ - 1 - 2 * place)


def prepare(pos, gate, up, cot, weight, basis, hidden, pack, both, plain):
    x, y, c = pos[0], pos[1], pos[2]
    for r in range(NX):
        block = lax.rem(x + r, NX) * 256
        for zl in range(NZ):
            piece = cot[:, pl.ds(pl.multiple_of(zl * 1024 + block, 256), 256)]
            for zh in range(NH):
                pack[zl * NH + zh, :, r * 256 : (r + 1) * 256] = piece
    both[:896, :] = weight[...]
    both[896:1152, :] = basis[:, :256]
    both[1152:, :] = basis[:, 256:]
    g = gate[...].astype(f32)
    plain[...] = g * jax.nn.sigmoid(g) * up[...].astype(f32)
    for cr in range(NC):
        for yr in range(NY):
            first = (lax.rem(y + yr, NY) * 4 + lax.rem(c + cr, NC)) * 8
            pair = [plain[pl.ds(pl.multiple_of(first + zh * 16, 8), 8), :] for zh in range(NH)]
            hidden[pl.ds((cr * NY + yr) * 16, 16), :] = jnp.concatenate(pair, 0).astype(bf16)


def backward(pos, *refs):
    cots, boths = refs[:8], refs[8:12]
    grad, reduced, tile = refs[12:]
    for piece in range(8):
        for zl in range(NZ):
            tile[pl.ds(zl * 128 + piece * 16, 16), :] = cots[piece][pl.ds(zl * 16, 16), :]

    def rows(step, _):
        at = pl.ds(pl.multiple_of(step * 256, 256), 256)
        total, left, right = None, None, None
        for r in range(NX):
            part = tile[at, r * 256 : (r + 1) * 256]
            more = dot(part, boths[r][:896, :], ((1,), (1,)))
            total = more if total is None else total + more
            more = dot(part, boths[r][896:1152, :], ((1,), (0,)))
            left = more if left is None else left + more
            more = dot(part, boths[r][1152:, :], ((1,), (0,)))
            right = more if right is None else right + more
        grad[at, :] = total.astype(bf16)
        reduced[at, :256] = left.astype(bf16)
        reduced[at, 256:] = right.astype(bf16)
        return 0

    lax.fori_loop(0, 4, rows, 0)


def project(pos, *refs):
    hiddens, reduced = refs[:8], refs[8]
    tile, outs, total, blocks = refs[9], refs[10:14], *refs[14:]
    x, zl_own = pos[0], pos[3]
    for hop in range(NZ):
        to = pl.ds(pl.multiple_of(ring_block(zl_own, hop) * 128, 128), 128)
        tile[to, :] = hiddens[hop][...]
    total[...] = dot(tile[...], reduced[...], ((0,), (0,)))
    spare = jnp.zeros((4, total.shape[1]), f32)
    for xs in range(NX):
        for zl in range(NZ):
            first = zl * 112 + xs * 28
            block = jnp.concatenate([total[first : first + 28, :], spare], 0)
            blocks[xs, zl * 32 : zl * 32 + 32, :] = block.astype(bf16)
    for xr, out in enumerate(outs):
        out[...] = blocks[lax.rem(x + xr, NX)]


def forward(pos, tile, b0, b1, b2, b3, o0, o1, o2, o3, leave):
    def rows(step, _):
        part = tile[pl.ds(pl.multiple_of(step * 256, 256), 256), :]
        for r, both in enumerate((b0, b1, b2, b3)):
            term = dot(part, both[:896, :], ((1,), (0,))).astype(bf16)
            for half in range(2):
                to = pl.ds(pl.multiple_of((step * 2 + half) * 16, 16), 16)
                for piece in range(8):
                    first = half * 128 + piece * 16
                    block = term[first : first + 16, :]
                    if piece < NY:
                        (o0, o1, o2, o3)[piece][to, r * 256 : (r + 1) * 256] = block
                    else:
                        leave[piece - NY, to, r * 256 : (r + 1) * 256] = block
        return 0

    lax.fori_loop(0, 4, rows, 0)


def finish_out(pos, parts, out):
    x = pos[0]
    for zl in range(NZ):
        both = (parts[zl * NH].astype(f32) + parts[zl * NH + 1].astype(f32)).astype(bf16)
        for r in range(NX):
            block = zl * 1024 + lax.rem(x + r, NX) * 256
            out[:, pl.ds(pl.multiple_of(block, 256), 256)] = both[:, r * 256 : (r + 1) * 256]


def finish_grad(pos, total, gate, up, grad_gate, grad_up, relative, plain):
    y, c = pos[1], pos[2]
    relative[...] = total[...].astype(f32)
    for ys in range(NY):
        yr = lax.rem(ys - y + NY, NY)
        for zh in range(NH):
            for cs in range(NC):
                cr = lax.rem(cs + c, NC)
                first = ((cr * NY + yr) * NH + zh) * 8
                to = ((ys * NH + zh) * NC + cs) * 8
                plain[to : to + 8, :] = relative[pl.ds(pl.multiple_of(first, 8), 8), :]
    g, u, d = gate[...].astype(f32), up[...].astype(f32), plain[...]
    s = jax.nn.sigmoid(g)
    grad_up[...] = (d * g * s).astype(bf16)
    grad_gate[...] = (d * u * s * (1.0 + g * (1.0 - s))).astype(bf16)


def expand(pos, s0, s1, s2, s3, basis, out, pieces, steps):
    x = pos[0]
    for xr, piece in enumerate((s0, s1, s2, s3)):
        pieces[lax.rem(x + xr, NX)] = piece[...].astype(f32)
    for xs in range(NX):
        for zl in range(NZ):
            first = zl * 112 + xs * 28
            steps[first : first + 28, :] = pieces[xs, zl * 32 : zl * 32 + 28, :]
    out[...] = dot(steps[...].astype(bf16), basis[...], ((1,), (1,)))


def body(gate, up, weight, basis, cotangent, moment1, moment2):
    pos = jnp.stack([lax.axis_index(a) for a in ("x", "y", "c", "zl")]).astype(jnp.int32)
    rows, ff = gate.shape
    mine, width = cotangent.shape
    cols = width // NZ
    deep, rank = basis.shape
    own, slot = moment1.shape[0], 32

    hidden, pack, both = call(
        prepare,
        5,
        [
            ((rows, ff), bf16),
            ((NZ * NH, mine, cols), bf16),
            ((ff + 2 * deep, deep), bf16),
        ],
        [((rows, ff), f32)],
    )(pos, gate, up, cotangent, weight, basis)

    got = lax.all_to_all(pack, ("zl", "zh"), 0, 0, tiled=True).reshape(rows, cols)
    boths = [both] + [shift(both, "x", NX, by) for by in range(1, NX)]
    got, *boths = lax.optimization_barrier((got, *boths))
    hiddens = [hidden]
    for _ in range(1, NZ - 2):
        hiddens.append(lax.ppermute(hiddens[-1], "zl", RING))
    cots = [got] + [shift(got, "y", NY, by) for by in range(1, NY)]
    cots = cots + [shift(piece, "c", NC, 1) for piece in cots]

    partial, reduced = call(
        backward,
        12,
        [((NZ * rows, ff), bf16), ((NZ * rows, rank), bf16)],
        [((NZ * rows, cols), bf16)],
        flops=3 * 10**9,
    )(pos, *cots, *boths)
    hiddens[-1], partial, reduced = lax.optimization_barrier((hiddens[-1], partial, reduced))
    for _ in range(2):
        hiddens.append(lax.ppermute(hiddens[-1], "zl", RING))
    grad_hidden = lax.psum_scatter(partial, "zl", scatter_dimension=0, tiled=True)
    grad_gate, grad_up = call(
        finish_grad,
        3,
        [((rows, ff), bf16), ((rows, ff), bf16)],
        [((rows, ff), f32), ((rows, ff), f32)],
    )(pos, grad_hidden, gate, up)

    tile, *parts = call(
        project,
        9,
        [((NZ * rows, ff), bf16)] + [((NZ * slot, rank), bf16)] * NX,
        [((ff, rank), f32), ((NX, NZ * slot, rank), bf16)],
        flops=10**9,
    )(pos, *hiddens, reduced)
    total = parts[0].astype(f32)
    for by in range(1, NX):
        total = total + shift(parts[by], "x", NX, -by).astype(f32)
    total, tile = lax.optimization_barrier((total.astype(bf16), tile))
    total = lax.all_to_all(total, "zl", 0, 0, tiled=True).reshape(NZ, slot, rank)
    projected = total.astype(f32).sum(0)[:own]
    moment1_new = 0.9 * moment1 + 0.1 * projected
    moment2_new = 0.999 * moment2 + 0.001 * projected * projected
    step = (moment1_new / corr_first / (jnp.sqrt(moment2_new / corr_second) + 1e-08)).astype(bf16)
    step = jnp.pad(step, ((0, slot - own), (0, 0)))
    *term, leave = call(
        forward, 5, [((rows, cols), bf16)] * NY + [((NY, rows, cols), bf16)], flops=2 * 10**9
    )(pos, tile, *boths)
    arrived = shift(leave, "c", NC, 1)
    term = [(term[yr].astype(f32) + arrived[yr].astype(f32)).astype(bf16) for yr in range(NY)]
    step, *term = lax.optimization_barrier((step, *term))
    step = jnp.broadcast_to(step[None], (NZ, slot, rank))
    step = lax.all_to_all(step, "zl", 0, 0, tiled=True).reshape(NZ * slot, rank)
    steps = [step] + [shift(step, "x", NX, by) for by in range(1, NX)]
    (expansion,) = call(
        expand,
        5,
        [((ff, deep), f32)],
        [((NX, NZ * slot, rank), f32), ((ff, rank), f32)],
        flops=3 * 10**8,
    )(pos, *steps, basis)

    total = term[0].astype(f32)
    for by in range(1, NY):
        total = total + shift(term[by], "y", NY, -by).astype(f32)
    total = total.astype(bf16).reshape(NZ * NH, mine, cols)
    total = lax.all_to_all(total, ("zl", "zh"), 0, 0, tiled=True)
    (layer_out,) = call(finish_out, 1, [((mine, width), bf16)])(pos, total)
    return (layer_out, grad_gate, grad_up, moment1_new, moment2_new, expansion)


def solution(mesh):
    fine = Mesh(mesh.devices.reshape(NZ, NX, NY, NH, NC), ("zl", "x", "y", "zh", "c"))
    dp, tensor = ("zl", "x"), ("y", "zh", "c")
    placed = (
        P(dp, tensor),
        P(dp, tensor),
        P(tensor, dp),
        P(dp, None),
        P(dp + tensor, None),
        P(tensor + dp, None),
        P(tensor + dp, None),
    )
    return jax.shard_map(
        body,
        mesh=fine,
        in_specs=placed,
        out_specs=(
            P(dp + tensor, None),
            P(dp, tensor),
            P(dp, tensor),
            P(tensor + dp, None),
            P(tensor + dp, None),
            P(tensor, dp),
        ),
        check_vma=False,
    )
```

```python
import jax
import jax.numpy as jnp
from jax import lax
from jax.experimental import pallas as pl
from jax.experimental.pallas import tpu as pltpu
from jax.sharding import Mesh, PartitionSpec as P

corr_first = 1.0 - 0.9**10
corr_second = 1.0 - 0.999**10

NZ, NX, NY, NH, NC = 8, 4, 4, 2, 2
bf16, f32 = jnp.bfloat16, jnp.float32
VMEM = pl.BlockSpec(memory_space=pltpu.VMEM)
SMEM = pl.BlockSpec(memory_space=pltpu.SMEM)
DMA = pltpu.SemaphoreType.DMA((6,))


def shift(value, axis, size, by):
    return lax.ppermute(value, axis, [(i, (i - by) % size) for i in range(size)])


def dot(a, b, contract):
    return lax.dot_general(a, b, (contract, ((), ())), preferred_element_type=f32)


def call(kernel, n_in, outs, scratch=(), flops=0, limit=20, place=VMEM):
    return pl.pallas_call(
        kernel,
        out_shape=tuple(jax.ShapeDtypeStruct(*o) for o in outs),
        in_specs=[SMEM] + [place] * n_in,
        out_specs=tuple(VMEM for _ in outs),
        scratch_shapes=[s if isinstance(s, type(DMA)) else pltpu.VMEM(*s) for s in scratch],
        compiler_params=pltpu.CompilerParams(vmem_limit_bytes=limit << 20),
        cost_estimate=pl.CostEstimate(flops=flops, bytes_accessed=4 << 20, transcendentals=0),
    )


def prepare(pos, gate, up, cot, weight, basis, hidden, pack, both, g_in, u_in, c_in, plain, sems):
    x, y, c = pos[0], pos[1], pos[2]
    moves = (
        (cot, c_in),
        (gate, g_in),
        (up, u_in),
        (weight, both.at[:896]),
        (basis.at[:, :256], both.at[896:1152]),
        (basis.at[:, 256:], both.at[1152:]),
    )
    copies = [pltpu.make_async_copy(a, b, sems.at[i]) for i, (a, b) in enumerate(moves)]
    for copy in copies:
        copy.start()
    copies[0].wait()
    for r in range(NX):
        block = lax.rem(x + r, NX) * 256
        for zl in range(NZ):
            piece = c_in[:, pl.ds(pl.multiple_of(zl * 1024 + block, 256), 256)]
            for zh in range(NH):
                pack[zl * NH + zh, :, r * 256 : (r + 1) * 256] = piece
    copies[1].wait()
    copies[2].wait()
    g = g_in[...].astype(f32)
    plain[...] = g * jax.nn.sigmoid(g) * u_in[...].astype(f32)
    for cr in range(NC):
        for yr in range(NY):
            first = (lax.rem(y + yr, NY) * 4 + lax.rem(c + cr, NC)) * 8
            pair = [plain[pl.ds(pl.multiple_of(first + zh * 16, 8), 8), :] for zh in range(NH)]
            hidden[pl.ds((cr * NY + yr) * 16, 16), :] = jnp.concatenate(pair, 0).astype(bf16)
    for copy in copies[3:]:
        copy.wait()


def backward(pos, *refs):
    cots, boths = refs[:8], refs[8:12]
    grad, reduced, tile = refs[12:]
    for piece in range(8):
        for zl in range(NZ):
            tile[pl.ds(zl * 128 + piece * 16, 16), :] = cots[piece][pl.ds(zl * 16, 16), :]

    def rows(step, _):
        at = pl.ds(pl.multiple_of(step * 256, 256), 256)
        total, left, right = None, None, None
        for r in range(NX):
            part = tile[at, r * 256 : (r + 1) * 256]
            more = dot(part, boths[r][:896, :], ((1,), (1,)))
            total = more if total is None else total + more
            more = dot(part, boths[r][896:1152, :], ((1,), (0,)))
            left = more if left is None else left + more
            more = dot(part, boths[r][1152:, :], ((1,), (0,)))
            right = more if right is None else right + more
        grad[at, :] = total.astype(bf16)
        reduced[at, :256] = left.astype(bf16)
        reduced[at, 256:] = right.astype(bf16)
        return 0

    lax.fori_loop(0, 4, rows, 0)


def project(pos, tile, reduced, o0, o1, o2, o3, total, blocks):
    x = pos[0]
    total[...] = dot(tile[...], reduced[...], ((0,), (0,)))
    spare = jnp.zeros((4, total.shape[1]), f32)
    for xs in range(NX):
        for zl in range(NZ):
            first = zl * 112 + xs * 28
            block = jnp.concatenate([total[first : first + 28, :], spare], 0)
            blocks[xs, zl * 32 : zl * 32 + 32, :] = block.astype(bf16)
    for xr, out in enumerate((o0, o1, o2, o3)):
        out[...] = blocks[lax.rem(x + xr, NX)]


def forward(pos, tile, b0, b1, b2, b3, o0, o1, o2, o3, leave):
    def rows(step, _):
        part = tile[pl.ds(pl.multiple_of(step * 256, 256), 256), :]
        for r, both in enumerate((b0, b1, b2, b3)):
            term = dot(part, both[:896, :], ((1,), (0,))).astype(bf16)
            for half in range(2):
                to = pl.ds(pl.multiple_of((step * 2 + half) * 16, 16), 16)
                for piece in range(8):
                    first = half * 128 + piece * 16
                    block = term[first : first + 16, :]
                    if piece < NY:
                        (o0, o1, o2, o3)[piece][to, r * 256 : (r + 1) * 256] = block
                    else:
                        leave[piece - NY, to, r * 256 : (r + 1) * 256] = block
        return 0

    lax.fori_loop(0, 4, rows, 0)


def finish_out(pos, parts, out):
    x = pos[0]
    for zl in range(NZ):
        both = (parts[zl * NH].astype(f32) + parts[zl * NH + 1].astype(f32)).astype(bf16)
        for r in range(NX):
            block = zl * 1024 + lax.rem(x + r, NX) * 256
            out[:, pl.ds(pl.multiple_of(block, 256), 256)] = both[:, r * 256 : (r + 1) * 256]


def finish_grad(pos, total, gate, up, grad_gate, grad_up, relative, plain):
    y, c = pos[1], pos[2]
    relative[...] = total[...].astype(f32)
    for ys in range(NY):
        yr = lax.rem(ys - y + NY, NY)
        for zh in range(NH):
            for cs in range(NC):
                cr = lax.rem(cs + c, NC)
                first = ((cr * NY + yr) * NH + zh) * 8
                to = ((ys * NH + zh) * NC + cs) * 8
                plain[to : to + 8, :] = relative[pl.ds(pl.multiple_of(first, 8), 8), :]
    g, u, d = gate[...].astype(f32), up[...].astype(f32), plain[...]
    s = jax.nn.sigmoid(g)
    grad_up[...] = (d * g * s).astype(bf16)
    grad_gate[...] = (d * u * s * (1.0 + g * (1.0 - s))).astype(bf16)


def expand(pos, s0, s1, s2, s3, basis, out, pieces, steps):
    x = pos[0]
    for xr, piece in enumerate((s0, s1, s2, s3)):
        pieces[lax.rem(x + xr, NX)] = piece[...].astype(f32)
    for xs in range(NX):
        for zl in range(NZ):
            first = zl * 112 + xs * 28
            steps[first : first + 28, :] = pieces[xs, zl * 32 : zl * 32 + 28, :]
    out[...] = dot(steps[...].astype(bf16), basis[...], ((1,), (1,)))


def body(gate, up, weight, basis, cotangent, moment1, moment2):
    pos = jnp.stack([lax.axis_index(a) for a in ("x", "y", "c")]).astype(jnp.int32)
    rows, ff = gate.shape
    mine, width = cotangent.shape
    cols = width // NZ
    deep, rank = basis.shape
    own, slot = moment1.shape[0], 32

    hidden, pack, both = call(
        prepare,
        5,
        [
            ((rows, ff), bf16),
            ((NZ * NH, mine, cols), bf16),
            ((ff + 2 * deep, deep), bf16),
        ],
        [
            ((rows, ff), bf16),
            ((rows, ff), bf16),
            ((mine, width), bf16),
            ((rows, ff), f32),
            DMA,
        ],
        place=pl.BlockSpec(memory_space=pl.ANY),
    )(pos, gate, up, cotangent, weight, basis)

    tile = lax.all_gather(hidden, "zl", axis=0, tiled=True)
    got = lax.all_to_all(pack, ("zl", "zh"), 0, 0, tiled=True).reshape(rows, cols)
    boths = [both] + [shift(both, "x", NX, by) for by in range(1, NX)]
    got, *boths = lax.optimization_barrier((got, *boths))
    cots = [got] + [shift(got, "y", NY, by) for by in range(1, NY)]
    cots = cots + [shift(piece, "c", NC, 1) for piece in cots]

    partial, reduced = call(
        backward,
        12,
        [((NZ * rows, ff), bf16), ((NZ * rows, rank), bf16)],
        [((NZ * rows, cols), bf16)],
        flops=3 * 10**9,
    )(pos, *cots, *boths)
    grad_hidden = lax.psum_scatter(partial, "zl", scatter_dimension=0, tiled=True)
    grad_gate, grad_up = call(
        finish_grad,
        3,
        [((rows, ff), bf16), ((rows, ff), bf16)],
        [((rows, ff), f32), ((rows, ff), f32)],
    )(pos, grad_hidden, gate, up)

    parts = call(
        project,
        2,
        [((NZ * slot, rank), bf16)] * NX,
        [((ff, rank), f32), ((NX, NZ * slot, rank), bf16)],
        flops=10**9,
    )(pos, tile, reduced)
    total = parts[0].astype(f32)
    for by in range(1, NX):
        total = total + shift(parts[by], "x", NX, -by).astype(f32)
    total, tile = lax.optimization_barrier((total.astype(bf16), tile))
    total = lax.all_to_all(total, "zl", 0, 0, tiled=True).reshape(NZ, slot, rank)
    projected = total.astype(f32).sum(0)[:own]
    moment1_new = 0.9 * moment1 + 0.1 * projected
    moment2_new = 0.999 * moment2 + 0.001 * projected * projected
    step = (moment1_new / corr_first / (jnp.sqrt(moment2_new / corr_second) + 1e-08)).astype(bf16)
    step = jnp.pad(step, ((0, slot - own), (0, 0)))
    *term, leave = call(
        forward, 5, [((rows, cols), bf16)] * NY + [((NY, rows, cols), bf16)], flops=2 * 10**9
    )(pos, tile, *boths)
    arrived = shift(leave, "c", NC, 1)
    term = [(term[yr].astype(f32) + arrived[yr].astype(f32)).astype(bf16) for yr in range(NY)]
    step, *term = lax.optimization_barrier((step, *term))
    step = jnp.broadcast_to(step[None], (NZ, slot, rank))
    step = lax.all_to_all(step, "zl", 0, 0, tiled=True).reshape(NZ * slot, rank)
    steps = [step] + [shift(step, "x", NX, by) for by in range(1, NX)]
    (expansion,) = call(
        expand,
        5,
        [((ff, deep), f32)],
        [((NX, NZ * slot, rank), f32), ((ff, rank), f32)],
        flops=3 * 10**8,
    )(pos, *steps, basis)

    total = term[0].astype(f32)
    for by in range(1, NY):
        total = total + shift(term[by], "y", NY, -by).astype(f32)
    total = total.astype(bf16).reshape(NZ * NH, mine, cols)
    total = lax.all_to_all(total, ("zl", "zh"), 0, 0, tiled=True)
    (layer_out,) = call(finish_out, 1, [((mine, width), bf16)])(pos, total)
    return (layer_out, grad_gate, grad_up, moment1_new, moment2_new, expansion)


def solution(mesh):
    fine = Mesh(mesh.devices.reshape(NZ, NX, NY, NH, NC), ("zl", "x", "y", "zh", "c"))
    dp, tensor = ("zl", "x"), ("y", "zh", "c")
    placed = (
        P(dp, tensor),
        P(dp, tensor),
        P(tensor, dp),
        P(dp, None),
        P(dp + tensor, None),
        P(tensor + dp, None),
        P(tensor + dp, None),
    )
    return jax.shard_map(
        body,
        mesh=fine,
        in_specs=placed,
        out_specs=(
            P(dp + tensor, None),
            P(dp, tensor),
            P(dp, tensor),
            P(tensor + dp, None),
            P(tensor + dp, None),
            P(tensor, dp),
        ),
        check_vma=False,
    )
```

```python
import jax
import jax.numpy as jnp
from jax import lax
from jax.experimental import pallas as pl
from jax.experimental.pallas import tpu as pltpu
from jax.sharding import Mesh, PartitionSpec as P

corr_first = 1.0 - 0.9**10
corr_second = 1.0 - 0.999**10

NZ, NX, NY, NH, NC = 8, 4, 4, 2, 2
bf16, f32 = jnp.bfloat16, jnp.float32
VMEM = pl.BlockSpec(memory_space=pltpu.VMEM)
SMEM = pl.BlockSpec(memory_space=pltpu.SMEM)


def shift(value, axis, size, by):
    return lax.ppermute(value, axis, [(i, (i - by) % size) for i in range(size)])


def dot(a, b, contract):
    return lax.dot_general(a, b, (contract, ((), ())), preferred_element_type=f32)


def call(kernel, n_in, outs, scratch=(), flops=0, limit=20):
    return pl.pallas_call(
        kernel,
        out_shape=tuple(jax.ShapeDtypeStruct(*o) for o in outs),
        in_specs=[SMEM] + [VMEM] * n_in,
        out_specs=tuple(VMEM for _ in outs),
        scratch_shapes=[pltpu.VMEM(*s) for s in scratch],
        compiler_params=pltpu.CompilerParams(vmem_limit_bytes=limit << 20),
        cost_estimate=pl.CostEstimate(flops=flops, bytes_accessed=4 << 20, transcendentals=0),
    )


def prepare(pos, gate, up, cot, weight, basis, hidden, pack, both, plain):
    x, y, c = pos[0], pos[1], pos[2]
    for r in range(NX):
        block = lax.rem(x + r, NX) * 256
        for zl in range(NZ):
            piece = cot[:, pl.ds(pl.multiple_of(zl * 1024 + block, 256), 256)]
            for zh in range(NH):
                pack[zl * NH + zh, :, r * 256 : (r + 1) * 256] = piece
    both[:896, :] = weight[...]
    both[896:1152, :] = basis[:, :256]
    both[1152:, :] = basis[:, 256:]
    g = gate[...].astype(f32)
    plain[...] = g * jax.nn.sigmoid(g) * up[...].astype(f32)
    for cr in range(NC):
        for yr in range(NY):
            first = (lax.rem(y + yr, NY) * 4 + lax.rem(c + cr, NC)) * 8
            pair = [plain[pl.ds(pl.multiple_of(first + zh * 16, 8), 8), :] for zh in range(NH)]
            hidden[pl.ds((cr * NY + yr) * 16, 16), :] = jnp.concatenate(pair, 0).astype(bf16)


def reduce(pos, *refs):
    cots, boths = refs[:8], refs[8:12]
    tile, reduced = refs[12:]
    for piece in range(8):
        for zl in range(NZ):
            tile[pl.ds(zl * 128 + piece * 16, 16), :] = cots[piece][pl.ds(zl * 16, 16), :]

    def rows(step, _):
        at = pl.ds(pl.multiple_of(step * 256, 256), 256)
        for side in range(2):
            total = None
            for r in range(NX):
                part = boths[r][896 + side * 256 : 1152 + side * 256, :]
                more = dot(tile[at, r * 256 : (r + 1) * 256], part, ((1,), (0,)))
                total = more if total is None else total + more
            reduced[at, side * 256 : (side + 1) * 256] = total.astype(bf16)
        return 0

    lax.fori_loop(0, 4, rows, 0)


def backward(pos, tile, b0, b1, b2, b3, grad):
    def rows(step, _):
        at = pl.ds(pl.multiple_of(step * 256, 256), 256)
        total = None
        for r, both in enumerate((b0, b1, b2, b3)):
            more = dot(tile[at, r * 256 : (r + 1) * 256], both[:896, :], ((1,), (1,)))
            total = more if total is None else total + more
        grad[at, :] = total.astype(bf16)
        return 0

    lax.fori_loop(0, 4, rows, 0)


def project(pos, tile, reduced, o0, o1, o2, o3, total, blocks):
    x = pos[0]
    total[...] = dot(tile[...], reduced[...], ((0,), (0,)))
    spare = jnp.zeros((4, total.shape[1]), f32)
    for xs in range(NX):
        for zl in range(NZ):
            first = zl * 112 + xs * 28
            block = jnp.concatenate([total[first : first + 28, :], spare], 0)
            blocks[xs, zl * 32 : zl * 32 + 32, :] = block.astype(bf16)
    for xr, out in enumerate((o0, o1, o2, o3)):
        out[...] = blocks[lax.rem(x + xr, NX)]


def forward(pos, tile, b0, b1, b2, b3, o0, o1, o2, o3, leave):
    def rows(step, _):
        part = tile[pl.ds(pl.multiple_of(step * 256, 256), 256), :]
        for r, both in enumerate((b0, b1, b2, b3)):
            term = dot(part, both[:896, :], ((1,), (0,))).astype(bf16)
            for half in range(2):
                to = pl.ds(pl.multiple_of((step * 2 + half) * 16, 16), 16)
                for piece in range(8):
                    first = half * 128 + piece * 16
                    block = term[first : first + 16, :]
                    if piece < NY:
                        (o0, o1, o2, o3)[piece][to, r * 256 : (r + 1) * 256] = block
                    else:
                        leave[piece - NY, to, r * 256 : (r + 1) * 256] = block
        return 0

    lax.fori_loop(0, 4, rows, 0)


def finish_out(pos, parts, out):
    x = pos[0]
    for zl in range(NZ):
        both = (parts[zl * NH].astype(f32) + parts[zl * NH + 1].astype(f32)).astype(bf16)
        for r in range(NX):
            block = zl * 1024 + lax.rem(x + r, NX) * 256
            out[:, pl.ds(pl.multiple_of(block, 256), 256)] = both[:, r * 256 : (r + 1) * 256]


def finish_grad(pos, total, gate, up, grad_gate, grad_up, relative, plain):
    y, c = pos[1], pos[2]
    relative[...] = total[...].astype(f32)
    for ys in range(NY):
        yr = lax.rem(ys - y + NY, NY)
        for zh in range(NH):
            for cs in range(NC):
                cr = lax.rem(cs + c, NC)
                first = ((cr * NY + yr) * NH + zh) * 8
                to = ((ys * NH + zh) * NC + cs) * 8
                plain[to : to + 8, :] = relative[pl.ds(pl.multiple_of(first, 8), 8), :]
    g, u, d = gate[...].astype(f32), up[...].astype(f32), plain[...]
    s = jax.nn.sigmoid(g)
    grad_up[...] = (d * g * s).astype(bf16)
    grad_gate[...] = (d * u * s * (1.0 + g * (1.0 - s))).astype(bf16)


def expand(pos, s0, s1, s2, s3, basis, out, pieces, steps):
    x = pos[0]
    for xr, piece in enumerate((s0, s1, s2, s3)):
        pieces[lax.rem(x + xr, NX)] = piece[...].astype(f32)
    for xs in range(NX):
        for zl in range(NZ):
            first = zl * 112 + xs * 28
            steps[first : first + 28, :] = pieces[xs, zl * 32 : zl * 32 + 28, :]
    out[...] = dot(steps[...].astype(bf16), basis[...], ((1,), (1,)))


def body(gate, up, weight, basis, cotangent, moment1, moment2):
    pos = jnp.stack([lax.axis_index(a) for a in ("x", "y", "c")]).astype(jnp.int32)
    rows, ff = gate.shape
    mine, width = cotangent.shape
    cols = width // NZ
    deep, rank = basis.shape
    own, slot = moment1.shape[0], 32

    hidden, pack, both = call(
        prepare,
        5,
        [
            ((rows, ff), bf16),
            ((NZ * NH, mine, cols), bf16),
            ((ff + 2 * deep, deep), bf16),
        ],
        [((rows, ff), f32)],
    )(pos, gate, up, cotangent, weight, basis)

    tile = lax.all_gather(hidden, "zl", axis=0, tiled=True)
    got = lax.all_to_all(pack, ("zl", "zh"), 0, 0, tiled=True).reshape(rows, cols)
    boths = [both] + [shift(both, "x", NX, by) for by in range(1, NX)]
    got, boths[1], boths[3] = lax.optimization_barrier((got, boths[1], boths[3]))
    cots = [got] + [shift(got, "y", NY, by) for by in range(1, NY)]
    cots = cots + [shift(piece, "c", NC, 1) for piece in cots]

    tile_cot, reduced = call(
        reduce,
        12,
        [((NZ * rows, cols), bf16), ((NZ * rows, rank), bf16)],
        flops=10**9,
    )(pos, *cots, *boths)

    parts = call(
        project,
        2,
        [((NZ * slot, rank), bf16)] * NX,
        [((ff, rank), f32), ((NX, NZ * slot, rank), bf16)],
        flops=10**9,
    )(pos, tile, reduced)
    tile_cot, *parts = lax.optimization_barrier((tile_cot, *parts))
    (partial,) = call(backward, 5, [((NZ * rows, ff), bf16)], flops=2 * 10**9)(
        pos, tile_cot, *boths
    )
    grad_hidden = lax.psum_scatter(partial, "zl", scatter_dimension=0, tiled=True)
    total = parts[0].astype(f32)
    for by in range(1, NX):
        total = total + shift(parts[by], "x", NX, -by).astype(f32)
    total, tile, partial = lax.optimization_barrier((total.astype(bf16), tile, partial))
    *term, leave = call(
        forward, 5, [((rows, cols), bf16)] * NY + [((NY, rows, cols), bf16)], flops=2 * 10**9
    )(pos, tile, *boths)
    arrived = shift(leave, "c", NC, 1)
    term = [(term[yr].astype(f32) + arrived[yr].astype(f32)).astype(bf16) for yr in range(NY)]
    outer = term[0].astype(f32)
    for by in range(1, NY):
        outer = outer + shift(term[by], "y", NY, -by).astype(f32)
    outer = outer.astype(bf16).reshape(NZ * NH, mine, cols)
    total = lax.all_to_all(total, "zl", 0, 0, tiled=True).reshape(NZ, slot, rank)
    projected = total.astype(f32).sum(0)[:own]
    moment1_new = 0.9 * moment1 + 0.1 * projected
    moment2_new = 0.999 * moment2 + 0.001 * projected * projected
    step = (moment1_new / corr_first / (jnp.sqrt(moment2_new / corr_second) + 1e-08)).astype(bf16)
    step = jnp.pad(step, ((0, slot - own), (0, 0)))
    step = jnp.broadcast_to(step[None], (NZ, slot, rank))
    step = lax.all_to_all(step, "zl", 0, 0, tiled=True).reshape(NZ * slot, rank)
    steps = [step] + [shift(step, "x", NX, by) for by in range(1, NX)]
    outer, steps[1] = lax.optimization_barrier((outer, steps[1]))
    (expansion,) = call(
        expand,
        5,
        [((ff, deep), f32)],
        [((NX, NZ * slot, rank), f32), ((ff, rank), f32)],
        flops=3 * 10**8,
    )(pos, *steps, basis)

    outer = lax.all_to_all(outer, ("zl", "zh"), 0, 0, tiled=True)
    (layer_out,) = call(finish_out, 1, [((mine, width), bf16)])(pos, outer)
    grad_gate, grad_up = call(
        finish_grad,
        3,
        [((rows, ff), bf16), ((rows, ff), bf16)],
        [((rows, ff), f32), ((rows, ff), f32)],
    )(pos, grad_hidden, gate, up)
    return (layer_out, grad_gate, grad_up, moment1_new, moment2_new, expansion)


def solution(mesh):
    fine = Mesh(mesh.devices.reshape(NZ, NX, NY, NH, NC), ("zl", "x", "y", "zh", "c"))
    dp, tensor = ("zl", "x"), ("y", "zh", "c")
    placed = (
        P(dp, tensor),
        P(dp, tensor),
        P(tensor, dp),
        P(dp, None),
        P(dp + tensor, None),
        P(tensor + dp, None),
        P(tensor + dp, None),
    )
    return jax.shard_map(
        body,
        mesh=fine,
        in_specs=placed,
        out_specs=(
            P(dp + tensor, None),
            P(dp, tensor),
            P(dp, tensor),
            P(tensor + dp, None),
            P(tensor + dp, None),
            P(tensor, dp),
        ),
        check_vma=False,
    )
```

```python
import jax
import jax.numpy as jnp
from jax import lax
from jax.experimental import pallas as pl
from jax.experimental.pallas import tpu as pltpu
from jax.sharding import Mesh, PartitionSpec as P

corr_first = 1.0 - 0.9**10
corr_second = 1.0 - 0.999**10

NA, NB, NX, NY, NH, NC = 2, 4, 4, 4, 2, 2
NZ = NA * NB
ORDER = (0, 1, 3, 2)
RING = [(ORDER[i], ORDER[(i + 1) % NB]) for i in range(NB)]
bf16, f32 = jnp.bfloat16, jnp.float32
VMEM = pl.BlockSpec(memory_space=pltpu.VMEM)
SMEM = pl.BlockSpec(memory_space=pltpu.SMEM)


def shift(value, axis, size, by):
    return lax.ppermute(value, axis, [(i, (i - by) % size) for i in range(size)])


def swap(value, axis):
    return lax.ppermute(value, axis, [(0, 1), (1, 0)])


def spread(value, axis, size):
    copies = jnp.broadcast_to(value[None], (size,) + value.shape)
    return lax.all_to_all(copies, axis, 0, 0, tiled=True)


def dot(a, b, contract):
    return lax.dot_general(a, b, (contract, ((), ())), preferred_element_type=f32)


def call(kernel, n_in, outs, scratch=(), flops=0, limit=20):
    return pl.pallas_call(
        kernel,
        out_shape=tuple(jax.ShapeDtypeStruct(*o) for o in outs),
        in_specs=[SMEM] + [VMEM] * n_in,
        out_specs=tuple(VMEM for _ in outs),
        scratch_shapes=[pltpu.VMEM(*s) for s in scratch],
        compiler_params=pltpu.CompilerParams(vmem_limit_bytes=limit << 20),
        cost_estimate=pl.CostEstimate(flops=flops, bytes_accessed=4 << 20, transcendentals=0),
    )


def ring_block(zb, hop):
    place = ((zb ^ (zb >> 1)) - hop) & (NB - 1)
    return place ^ (place >> 1)


def prepare(pos, gate, up, cot, weight, basis, hidden, pack, both, plain):
    c = pos[3]
    for za in range(NA):
        for x in range(NX):
            for r in range(NB):
                block = ((za * NB + ring_block(pos[4], r)) * NX + x) * 256
                piece = cot[:, pl.ds(pl.multiple_of(block, 256), 256)]
                for zh in range(NH):
                    pack[(za * NX + x) * NH + zh, :, r * 256 : (r + 1) * 256] = piece
    both[:896, :] = weight[...]
    both[896:1152, :] = basis[:, :256]
    both[1152:, :] = basis[:, 256:]
    g = gate[...].astype(f32)
    plain[...] = g * jax.nn.sigmoid(g) * up[...].astype(f32)
    for cr in range(NC):
        for y in range(NY):
            first = (y * 4 + lax.rem(c + cr, NC)) * 8
            pair = [plain[pl.ds(pl.multiple_of(first + zh * 16, 8), 8), :] for zh in range(NH)]
            hidden[pl.ds((cr * NY + y) * 16, 16), :] = jnp.concatenate(pair, 0).astype(bf16)


def project(pos, *refs):
    cots, boths, hiddens = refs[:2], refs[2:6], refs[6:10]
    tile, out, reduced, total = refs[10:]
    za, x = pos[0], pos[1]
    for xr in range(NX):
        for ar in range(NA):
            at = (lax.rem(za + ar, NA) * NX + lax.rem(x + xr, NX)) * 16
            at = pl.ds(pl.multiple_of(at, 16), 16)
            for piece in range(8):
                to = (xr * NA + ar) * 128 + piece * 16
                tile[to : to + 16, :] = cots[piece // NY][piece % NY, at, :]

    def rows(step, _):
        at = pl.ds(pl.multiple_of(step * 256, 256), 256)
        for side in range(2):
            low = None
            for r in range(NB):
                part = boths[r][896 + side * 256 : 1152 + side * 256, :]
                more = dot(tile[at, r * 256 : (r + 1) * 256], part, ((1,), (0,)))
                low = more if low is None else low + more
            reduced[at, side * 256 : (side + 1) * 256] = low.astype(bf16)
        return 0

    lax.fori_loop(0, 4, rows, 0)
    for xr in range(NX):
        more = dot(hiddens[xr][...], reduced[xr * 256 : (xr + 1) * 256, :], ((0,), (0,)))
        total[...] = more if xr == 0 else total[...] + more
    spare = jnp.zeros((4, total.shape[1]), f32)
    for xs in range(NX):
        for zl in range(NZ):
            first = zl * 112 + xs * 28
            block = jnp.concatenate([total[first : first + 28, :], spare], 0)
            out[xs, zl * 32 : zl * 32 + 32, :] = block.astype(bf16)


def backward(pos, tile, b0, b1, b2, b3, *outs):
    for xr, out in enumerate(outs):
        total = None
        for r, both in enumerate((b0, b1, b2, b3)):
            part = tile[xr * 256 : (xr + 1) * 256, r * 256 : (r + 1) * 256]
            more = dot(part, both[:896, :], ((1,), (1,)))
            total = more if total is None else total + more
        out[...] = total.astype(bf16)


def forward(pos, b0, b1, b2, b3, h0, h1, h2, h3, o0, o1, o2, o3, leave, stay):
    za, x, y = pos[0], pos[1], pos[2]
    for xr, hidden in enumerate((h0, h1, h2, h3)):
        for r, both in enumerate((b0, b1, b2, b3)):
            term = dot(hidden[...], both[:896, :], ((1,), (0,))).astype(bf16)
            for ar in range(NA):
                to = (lax.rem(za + ar, NA) * NX + lax.rem(x + xr, NX)) * 16
                to = pl.ds(pl.multiple_of(to, 16), 16)
                for piece in range(8):
                    first = ar * 128 + piece * 16
                    block = term[first : first + 16, :]
                    side = (stay, leave)[piece // NY]
                    side[lax.rem(piece % NY - y + NY, NY), to, r * 256 : (r + 1) * 256] = block
    for yr, out in enumerate((o0, o1, o2, o3)):
        out[...] = stay[yr]


def finish_out(pos, parts, out):
    for za in range(NA):
        for x in range(NX):
            at = (za * NX + x) * NH
            pair = (parts[at].astype(f32) + parts[at + 1].astype(f32)).astype(bf16)
            for r in range(NB):
                block = ((za * NB + ring_block(pos[4], r)) * NX + x) * 256
                to = pl.ds(pl.multiple_of(block, 256), 256)
                out[:, to] = pair[:, r * 256 : (r + 1) * 256]


def finish_grad(pos, p0, p1, p2, p3, arrived, gate, up, grad_gate, grad_up, relative, plain):
    c = pos[3]
    total = arrived[...].astype(f32)
    for part in (p0, p1, p2, p3):
        total = total + part[:128, :].astype(f32)
    relative[...] = total
    for ys in range(NY):
        for zh in range(NH):
            for cs in range(NC):
                cr = lax.rem(cs + c, NC)
                first = ((cr * NY + ys) * NH + zh) * 8
                to = ((ys * NH + zh) * NC + cs) * 8
                plain[to : to + 8, :] = relative[pl.ds(pl.multiple_of(first, 8), 8), :]
    g, u, d = gate[...].astype(f32), up[...].astype(f32), plain[...]
    s = jax.nn.sigmoid(g)
    grad_up[...] = (d * g * s).astype(bf16)
    grad_gate[...] = (d * u * s * (1.0 + g * (1.0 - s))).astype(bf16)


def expand(pos, s0, s1, s2, s3, basis, out, pieces, steps):
    x = pos[1]
    for xr, piece in enumerate((s0, s1, s2, s3)):
        pieces[lax.rem(x + xr, NX)] = piece[...].astype(f32)
    for xs in range(NX):
        for zl in range(NZ):
            first = zl * 112 + xs * 28
            steps[first : first + 28, :] = pieces[xs, zl * 32 : zl * 32 + 28, :]
    out[...] = dot(steps[...].astype(bf16), basis[...], ((1,), (1,)))


def body(gate, up, weight, basis, cotangent, moment1, moment2):
    pos = jnp.stack([lax.axis_index(a) for a in ("za", "x", "y", "c", "zb")]).astype(jnp.int32)
    rows, ff = gate.shape
    mine, width = cotangent.shape
    deep, rank = basis.shape
    cols = NB * deep
    own, slot = moment1.shape[0], 32
    square = ("za", "x", "zh")
    line = ("za", "zb")

    hidden, pack, both = call(
        prepare,
        5,
        [
            ((rows, ff), bf16),
            ((NA * NX * NH, mine, cols), bf16),
            ((ff + 2 * deep, deep), bf16),
        ],
        [((rows, ff), f32)],
    )(pos, gate, up, cotangent, weight, basis)

    cot = lax.all_to_all(pack, square, 0, 0, tiled=True).reshape(rows, cols)
    boths = [both, lax.ppermute(both, "zb", RING)]
    twin = swap(hidden, "za")
    cot, boths[1], twin = lax.optimization_barrier((cot, boths[1], twin))
    pair = jnp.concatenate([hidden, twin], 0)
    boths.append(lax.ppermute(boths[1], "zb", RING))
    cot = spread(cot, "y", NY)
    cot, boths[2] = lax.optimization_barrier((cot, boths[2]))
    boths.append(lax.ppermute(boths[2], "zb", RING))
    hiddens = [pair] + [shift(pair, "x", NX, by) for by in range(1, NX)]

    tile, parts = call(
        project,
        10,
        [((NX * NA * rows, cols), bf16), ((NX, NZ * slot, rank), bf16)],
        [((NX * NA * rows, rank), bf16), ((ff, rank), f32)],
        flops=2 * 10**9,
    )(pos, cot, swap(cot, "c"), *boths, *hiddens)
    tile, parts = lax.optimization_barrier((tile, parts))

    partial = call(backward, 5, [((NA * rows, ff), bf16)] * NX, flops=2 * 10**9)(
        pos, tile, *boths
    )
    partials = [partial[0]] + [shift(partial[by], "x", NX, -by) for by in range(1, NX)]
    leave = partials[0][rows:].astype(f32)
    for part in partials[1:]:
        leave = leave + part[rows:].astype(f32)
    leave = leave.astype(bf16)

    total = lax.all_to_all(parts, "x", 0, 0, tiled=True).astype(f32).sum(0).astype(bf16)
    total, leave, *hiddens = lax.optimization_barrier((total, leave, *hiddens))
    arrived = swap(leave, "za")
    *term, leave = call(
        forward,
        8,
        [((rows, cols), bf16)] * NY + [((NY, rows, cols), bf16)],
        [((NY, rows, cols), bf16)],
        flops=2 * 10**9,
    )(pos, *boths, *hiddens)
    other = swap(leave, "c")
    term = [(term[yr].astype(f32) + other[yr].astype(f32)).astype(bf16) for yr in range(NY)]
    outer = term[0].astype(f32)
    for by in range(1, NY):
        outer = outer + shift(term[by], "y", NY, -by).astype(f32)
    outer = outer.astype(bf16).reshape(NA * NX * NH, mine, cols)
    total = lax.all_to_all(total, line, 0, 0, tiled=True).reshape(NZ, slot, rank)
    projected = total.astype(f32).sum(0)[:own]
    moment1_new = 0.9 * moment1 + 0.1 * projected
    moment2_new = 0.999 * moment2 + 0.001 * projected * projected
    step = (moment1_new / corr_first / (jnp.sqrt(moment2_new / corr_second) + 1e-08)).astype(bf16)
    step = jnp.pad(step, ((0, slot - own), (0, 0)))
    step = jnp.broadcast_to(step[None], (NZ, slot, rank))
    step = lax.all_to_all(step, line, 0, 0, tiled=True).reshape(NZ * slot, rank)
    steps = [step] + [shift(step, "x", NX, by) for by in range(1, NX)]
    outer, steps[1] = lax.optimization_barrier((outer, steps[1]))
    (expansion,) = call(
        expand,
        5,
        [((ff, deep), f32)],
        [((NX, NZ * slot, rank), f32), ((ff, rank), f32)],
        flops=3 * 10**8,
    )(pos, *steps, basis)

    grad_gate, grad_up = call(
        finish_grad,
        7,
        [((rows, ff), bf16), ((rows, ff), bf16)],
        [((rows, ff), f32), ((rows, ff), f32)],
    )(pos, *partials, arrived, gate, up)

    outer = lax.all_to_all(outer, square, 0, 0, tiled=True)
    (layer_out,) = call(finish_out, 1, [((mine, width), bf16)])(pos, outer)
    return (layer_out, grad_gate, grad_up, moment1_new, moment2_new, expansion)


def solution(mesh):
    names = ("za", "zb", "x", "y", "zh", "c")
    fine = Mesh(mesh.devices.reshape(NA, NB, NX, NY, NH, NC), names)
    dp, tensor = ("za", "zb", "x"), ("y", "zh", "c")
    placed = (
        P(dp, tensor),
        P(dp, tensor),
        P(tensor, dp),
        P(dp, None),
        P(dp + tensor, None),
        P(tensor + dp, None),
        P(tensor + dp, None),
    )
    return jax.shard_map(
        body,
        mesh=fine,
        in_specs=placed,
        out_specs=(
            P(dp + tensor, None),
            P(dp, tensor),
            P(dp, tensor),
            P(tensor + dp, None),
            P(tensor + dp, None),
            P(tensor, dp),
        ),
        check_vma=False,
    )
```

```python
import jax
import jax.numpy as jnp
from jax import lax
from jax.experimental import pallas as pl
from jax.experimental.pallas import tpu as pltpu
from jax.sharding import Mesh, PartitionSpec as P

corr_first = 1.0 - 0.9**10
corr_second = 1.0 - 0.999**10

NZ, NX, NY, NH, NC = 8, 4, 4, 2, 2
bf16, f32 = jnp.bfloat16, jnp.float32
VMEM = pl.BlockSpec(memory_space=pltpu.VMEM)
SMEM = pl.BlockSpec(memory_space=pltpu.SMEM)


def shift(value, axis, size, by):
    return lax.ppermute(value, axis, [(i, (i - by) % size) for i in range(size)])


def dot(a, b, contract):
    return lax.dot_general(a, b, (contract, ((), ())), preferred_element_type=f32)


def call(kernel, n_in, outs, scratch=(), flops=0, limit=20):
    return pl.pallas_call(
        kernel,
        out_shape=tuple(jax.ShapeDtypeStruct(*o) for o in outs),
        in_specs=[SMEM] + [VMEM] * n_in,
        out_specs=tuple(VMEM for _ in outs),
        scratch_shapes=[pltpu.VMEM(*s) for s in scratch],
        compiler_params=pltpu.CompilerParams(vmem_limit_bytes=limit << 20),
        cost_estimate=pl.CostEstimate(flops=flops, bytes_accessed=4 << 20, transcendentals=0),
    )


def prepare(pos, gate, up, cot, weight, basis, hidden, pack, both, plain):
    x, y, c = pos[0], pos[1], pos[2]
    for r in range(NX):
        block = lax.rem(x + r, NX) * 256
        for zl in range(NZ):
            piece = cot[:, pl.ds(pl.multiple_of(zl * 1024 + block, 256), 256)]
            for zh in range(NH):
                pack[zl * NH + zh, :, r * 256 : (r + 1) * 256] = piece
    both[:896, :] = weight[...]
    both[896:1152, :] = basis[:, :256]
    both[1152:, :] = basis[:, 256:]
    g = gate[...].astype(f32)
    plain[...] = g * jax.nn.sigmoid(g) * up[...].astype(f32)
    for cr in range(NC):
        for yr in range(NY):
            first = (lax.rem(y + yr, NY) * 4 + lax.rem(c + cr, NC)) * 8
            pair = [plain[pl.ds(pl.multiple_of(first + zh * 16, 8), 8), :] for zh in range(NH)]
            hidden[pl.ds((cr * NY + yr) * 16, 16), :] = jnp.concatenate(pair, 0).astype(bf16)


def backward(pos, *refs):
    cots, boths = refs[:8], refs[8:12]
    grad, reduced, tile = refs[12:]
    for piece in range(8):
        for zl in range(NZ):
            tile[pl.ds(zl * 128 + piece * 16, 16), :] = cots[piece][pl.ds(zl * 16, 16), :]

    def rows(step, _):
        at = pl.ds(pl.multiple_of(step * 256, 256), 256)
        total, left, right = None, None, None
        for r in range(NX):
            part = tile[at, r * 256 : (r + 1) * 256]
            more = dot(part, boths[r][:896, :], ((1,), (1,)))
            total = more if total is None else total + more
            more = dot(part, boths[r][896:1152, :], ((1,), (0,)))
            left = more if left is None else left + more
            more = dot(part, boths[r][1152:, :], ((1,), (0,)))
            right = more if right is None else right + more
        grad[at, :] = total.astype(bf16)
        reduced[at, :256] = left.astype(bf16)
        reduced[at, 256:] = right.astype(bf16)
        return 0

    lax.fori_loop(0, 4, rows, 0)


def project(pos, tile, reduced, o0, o1, o2, o3, total, blocks):
    x = pos[0]
    total[...] = dot(tile[...], reduced[...], ((0,), (0,)))
    spare = jnp.zeros((4, total.shape[1]), f32)
    for xs in range(NX):
        for zl in range(NZ):
            first = zl * 112 + xs * 28
            block = jnp.concatenate([total[first : first + 28, :], spare], 0)
            blocks[xs, zl * 32 : zl * 32 + 32, :] = block.astype(bf16)
    for xr, out in enumerate((o0, o1, o2, o3)):
        out[...] = blocks[lax.rem(x + xr, NX)]


def forward(pos, tile, b0, b1, b2, b3, o0, o1, o2, o3, leave):
    def rows(step, _):
        part = tile[pl.ds(pl.multiple_of(step * 256, 256), 256), :]
        for r, both in enumerate((b0, b1, b2, b3)):
            term = dot(part, both[:896, :], ((1,), (0,))).astype(bf16)
            for half in range(2):
                to = pl.ds(pl.multiple_of((step * 2 + half) * 16, 16), 16)
                for piece in range(8):
                    first = half * 128 + piece * 16
                    block = term[first : first + 16, :]
                    if piece < NY:
                        (o0, o1, o2, o3)[piece][to, r * 256 : (r + 1) * 256] = block
                    else:
                        leave[piece - NY, to, r * 256 : (r + 1) * 256] = block
        return 0

    lax.fori_loop(0, 4, rows, 0)


def finish_out(pos, parts, out):
    x = pos[0]
    for zl in range(NZ):
        both = (parts[zl * NH].astype(f32) + parts[zl * NH + 1].astype(f32)).astype(bf16)
        for r in range(NX):
            block = zl * 1024 + lax.rem(x + r, NX) * 256
            out[:, pl.ds(pl.multiple_of(block, 256), 256)] = both[:, r * 256 : (r + 1) * 256]


def finish_grad(pos, total, gate, up, grad_gate, grad_up, relative, plain):
    y, c = pos[1], pos[2]
    relative[...] = total[...].astype(f32)
    for ys in range(NY):
        yr = lax.rem(ys - y + NY, NY)
        for zh in range(NH):
            for cs in range(NC):
                cr = lax.rem(cs + c, NC)
                first = ((cr * NY + yr) * NH + zh) * 8
                to = ((ys * NH + zh) * NC + cs) * 8
                plain[to : to + 8, :] = relative[pl.ds(pl.multiple_of(first, 8), 8), :]
    g, u, d = gate[...].astype(f32), up[...].astype(f32), plain[...]
    s = jax.nn.sigmoid(g)
    grad_up[...] = (d * g * s).astype(bf16)
    grad_gate[...] = (d * u * s * (1.0 + g * (1.0 - s))).astype(bf16)


def expand(pos, s0, s1, s2, s3, basis, out, pieces, steps):
    x = pos[0]
    for xr, piece in enumerate((s0, s1, s2, s3)):
        pieces[lax.rem(x + xr, NX)] = piece[...].astype(f32)
    for xs in range(NX):
        for zl in range(NZ):
            first = zl * 112 + xs * 28
            steps[first : first + 28, :] = pieces[xs, zl * 32 : zl * 32 + 28, :]
    out[...] = dot(steps[...].astype(bf16), basis[...], ((1,), (1,)))


def body(gate, up, weight, basis, cotangent, moment1, moment2):
    pos = jnp.stack([lax.axis_index(a) for a in ("x", "y", "c")]).astype(jnp.int32)
    rows, ff = gate.shape
    mine, width = cotangent.shape
    cols = width // NZ
    deep, rank = basis.shape
    own, slot = moment1.shape[0], 32

    hidden, pack, both = call(
        prepare,
        5,
        [
            ((rows, ff), bf16),
            ((NZ * NH, mine, cols), bf16),
            ((ff + 2 * deep, deep), bf16),
        ],
        [((rows, ff), f32)],
    )(pos, gate, up, cotangent, weight, basis)

    tile = lax.all_gather(hidden, "zl", axis=0, tiled=True)
    got = lax.all_to_all(pack, ("zl", "zh"), 0, 0, tiled=True).reshape(rows, cols)
    boths = [both, shift(both, "x", NX, 1), both, shift(both, "x", NX, 3)]
    got, *boths = lax.optimization_barrier((got, *boths))
    boths[2] = shift(boths[2], "x", NX, 2)
    cots = [got] + [shift(got, "y", NY, by) for by in range(1, NY)]
    cots = cots + [shift(piece, "c", NC, 1) for piece in cots]

    partial, reduced = call(
        backward,
        12,
        [((NZ * rows, ff), bf16), ((NZ * rows, rank), bf16)],
        [((NZ * rows, cols), bf16)],
        flops=3 * 10**9,
    )(pos, *cots, *boths)
    grad_hidden = lax.psum_scatter(partial, "zl", scatter_dimension=0, tiled=True)
    parts = call(
        project,
        2,
        [((NZ * slot, rank), bf16)] * NX,
        [((ff, rank), f32), ((NX, NZ * slot, rank), bf16)],
        flops=10**9,
    )(pos, tile, reduced)
    *term, leave = call(
        forward, 5, [((rows, cols), bf16)] * NY + [((NY, rows, cols), bf16)], flops=2 * 10**9
    )(pos, tile, *boths)
    leave, *parts = lax.optimization_barrier((leave, *parts))
    arrived = shift(leave, "c", NC, 1)
    term = [(term[yr].astype(f32) + arrived[yr].astype(f32)).astype(bf16) for yr in range(NY)]
    total = parts[0].astype(f32)
    for by in range(1, NX):
        total = total + shift(parts[by], "x", NX, -by).astype(f32)
    total, grad_hidden, *term = lax.optimization_barrier((total.astype(bf16), grad_hidden, *term))
    outer = term[0].astype(f32)
    for by in range(1, NY):
        outer = outer + shift(term[by], "y", NY, -by).astype(f32)
    outer = outer.astype(bf16).reshape(NZ * NH, mine, cols)
    total = lax.all_to_all(total, "zl", 0, 0, tiled=True).reshape(NZ, slot, rank)
    projected = total.astype(f32).sum(0)[:own]
    moment1_new = 0.9 * moment1 + 0.1 * projected
    moment2_new = 0.999 * moment2 + 0.001 * projected * projected
    step = (moment1_new / corr_first / (jnp.sqrt(moment2_new / corr_second) + 1e-08)).astype(bf16)
    step = jnp.pad(step, ((0, slot - own), (0, 0)))
    step = jnp.broadcast_to(step[None], (NZ, slot, rank))
    step = lax.all_to_all(step, "zl", 0, 0, tiled=True).reshape(NZ * slot, rank)
    steps = [step] + [shift(step, "x", NX, by) for by in range(1, NX)]
    outer, steps[1] = lax.optimization_barrier((outer, steps[1]))
    (expansion,) = call(
        expand,
        5,
        [((ff, deep), f32)],
        [((NX, NZ * slot, rank), f32), ((ff, rank), f32)],
        flops=3 * 10**8,
    )(pos, *steps, basis)

    outer = lax.all_to_all(outer, ("zl", "zh"), 0, 0, tiled=True)
    (layer_out,) = call(finish_out, 1, [((mine, width), bf16)])(pos, outer)
    grad_gate, grad_up = call(
        finish_grad,
        3,
        [((rows, ff), bf16), ((rows, ff), bf16)],
        [((rows, ff), f32), ((rows, ff), f32)],
    )(pos, grad_hidden, gate, up)
    return (layer_out, grad_gate, grad_up, moment1_new, moment2_new, expansion)


def solution(mesh):
    fine = Mesh(mesh.devices.reshape(NZ, NX, NY, NH, NC), ("zl", "x", "y", "zh", "c"))
    dp, tensor = ("zl", "x"), ("y", "zh", "c")
    placed = (
        P(dp, tensor),
        P(dp, tensor),
        P(tensor, dp),
        P(dp, None),
        P(dp + tensor, None),
        P(tensor + dp, None),
        P(tensor + dp, None),
    )
    return jax.shard_map(
        body,
        mesh=fine,
        in_specs=placed,
        out_specs=(
            P(dp + tensor, None),
            P(dp, tensor),
            P(dp, tensor),
            P(tensor + dp, None),
            P(tensor + dp, None),
            P(tensor, dp),
        ),
        check_vma=False,
    )
```

```python
import jax
import jax.numpy as jnp
from jax import lax
from jax.experimental import pallas as pl
from jax.experimental.pallas import tpu as pltpu
from jax.sharding import Mesh, PartitionSpec as P

corr_first = 1.0 - 0.9**10
corr_second = 1.0 - 0.999**10

NZ, NX, NY, NH, NC = 8, 4, 4, 2, 2
ORDER = (0, 2, 4, 6, 7, 5, 3, 1)
bf16, f32 = jnp.bfloat16, jnp.float32
VMEM = pl.BlockSpec(memory_space=pltpu.VMEM)
SMEM = pl.BlockSpec(memory_space=pltpu.SMEM)


def shift(value, axis, size, by):
    return lax.ppermute(value, axis, [(i, (i - by) % size) for i in range(size)])


def dot(a, b, contract):
    return lax.dot_general(a, b, (contract, ((), ())), preferred_element_type=f32)


def call(kernel, n_in, outs, scratch=(), flops=0, limit=20):
    return pl.pallas_call(
        kernel,
        out_shape=tuple(jax.ShapeDtypeStruct(*o) for o in outs),
        in_specs=[SMEM] + [VMEM] * n_in,
        out_specs=tuple(VMEM for _ in outs),
        scratch_shapes=[pltpu.VMEM(*s) for s in scratch],
        compiler_params=pltpu.CompilerParams(vmem_limit_bytes=limit << 20),
        cost_estimate=pl.CostEstimate(flops=flops, bytes_accessed=4 << 20, transcendentals=0),
    )


def prepare(pos, gate, up, cot, weight, basis, hidden, pack, both, plain):
    x, y, c = pos[0], pos[1], pos[2]
    for r in range(NX):
        block = lax.rem(x + r, NX) * 256
        for zl in range(NZ):
            piece = cot[:, pl.ds(pl.multiple_of(zl * 1024 + block, 256), 256)]
            for zh in range(NH):
                pack[zl * NH + zh, :, r * 256 : (r + 1) * 256] = piece
    both[:896, :] = weight[...]
    both[896:1152, :] = basis[:, :256]
    both[1152:, :] = basis[:, 256:]
    g = gate[...].astype(f32)
    plain[...] = g * jax.nn.sigmoid(g) * up[...].astype(f32)
    for cr in range(NC):
        for yr in range(NY):
            first = (lax.rem(y + yr, NY) * 4 + lax.rem(c + cr, NC)) * 8
            pair = [plain[pl.ds(pl.multiple_of(first + zh * 16, 8), 8), :] for zh in range(NH)]
            hidden[pl.ds((cr * NY + yr) * 16, 16), :] = jnp.concatenate(pair, 0).astype(bf16)


def backward(pos, *refs):
    cots, boths = refs[:8], refs[8:12]
    grad, reduced, tile = refs[12:]
    for piece in range(8):
        for at, zl in enumerate(ORDER):
            tile[pl.ds(at * 128 + piece * 16, 16), :] = cots[piece][pl.ds(zl * 16, 16), :]

    def rows(step, _):
        at = pl.ds(pl.multiple_of(step * 256, 256), 256)
        total, left, right = None, None, None
        for r in range(NX):
            part = tile[at, r * 256 : (r + 1) * 256]
            more = dot(part, boths[r][:896, :], ((1,), (1,)))
            total = more if total is None else total + more
            more = dot(part, boths[r][896:1152, :], ((1,), (0,)))
            left = more if left is None else left + more
            more = dot(part, boths[r][1152:, :], ((1,), (0,)))
            right = more if right is None else right + more
        grad[at, :] = total.astype(bf16)
        reduced[at, :256] = left.astype(bf16)
        reduced[at, 256:] = right.astype(bf16)
        return 0

    lax.fori_loop(0, 4, rows, 0)


def project(pos, tile, reduced, out, total):
    total[...] = dot(tile[...], reduced[...], ((0,), (0,)))
    spare = jnp.zeros((4, total.shape[1]), f32)
    for xs in range(NX):
        for zl in range(NZ):
            first = zl * 112 + xs * 28
            block = jnp.concatenate([total[first : first + 28, :], spare], 0)
            out[xs, zl * 32 : zl * 32 + 32, :] = block.astype(bf16)


def forward(pos, tile, b0, b1, b2, b3, o0, o1, o2, o3, leave):
    for step in range(4):
        part = tile[step * 256 : (step + 1) * 256, :]
        for r, both in enumerate((b0, b1, b2, b3)):
            term = dot(part, both[:896, :], ((1,), (0,))).astype(bf16)
            for half in range(2):
                zl = ORDER[step * 2 + half]
                to = pl.ds(zl * 16, 16)
                for piece in range(8):
                    first = half * 128 + piece * 16
                    block = term[first : first + 16, :]
                    if piece < NY:
                        (o0, o1, o2, o3)[piece][to, r * 256 : (r + 1) * 256] = block
                    else:
                        leave[piece - NY, to, r * 256 : (r + 1) * 256] = block


def finish_out(pos, parts, out):
    x = pos[0]
    for zl in range(NZ):
        both = (parts[zl * NH].astype(f32) + parts[zl * NH + 1].astype(f32)).astype(bf16)
        for r in range(NX):
            block = zl * 1024 + lax.rem(x + r, NX) * 256
            out[:, pl.ds(pl.multiple_of(block, 256), 256)] = both[:, r * 256 : (r + 1) * 256]


def finish_grad(pos, total, gate, up, grad_gate, grad_up, relative, plain):
    y, c = pos[1], pos[2]
    relative[...] = total[...].astype(f32)
    for ys in range(NY):
        yr = lax.rem(ys - y + NY, NY)
        for zh in range(NH):
            for cs in range(NC):
                cr = lax.rem(cs + c, NC)
                first = ((cr * NY + yr) * NH + zh) * 8
                to = ((ys * NH + zh) * NC + cs) * 8
                plain[to : to + 8, :] = relative[pl.ds(pl.multiple_of(first, 8), 8), :]
    g, u, d = gate[...].astype(f32), up[...].astype(f32), plain[...]
    s = jax.nn.sigmoid(g)
    grad_up[...] = (d * g * s).astype(bf16)
    grad_gate[...] = (d * u * s * (1.0 + g * (1.0 - s))).astype(bf16)


def expand(pos, s0, s1, s2, s3, basis, out, pieces, steps):
    x = pos[0]
    for xr, piece in enumerate((s0, s1, s2, s3)):
        pieces[lax.rem(x + xr, NX)] = piece[...].astype(f32)
    for xs in range(NX):
        for zl in range(NZ):
            first = zl * 112 + xs * 28
            steps[first : first + 28, :] = pieces[xs, zl * 32 : zl * 32 + 28, :]
    out[...] = dot(steps[...].astype(bf16), basis[...], ((1,), (1,)))


def body(gate, up, weight, basis, cotangent, moment1, moment2):
    pos = jnp.stack([lax.axis_index(a) for a in ("x", "y", "c")]).astype(jnp.int32)
    rows, ff = gate.shape
    mine, width = cotangent.shape
    cols = width // NZ
    deep, rank = basis.shape
    own, slot = moment1.shape[0], 32

    hidden, pack, both = call(
        prepare,
        5,
        [
            ((rows, ff), bf16),
            ((NZ * NH, mine, cols), bf16),
            ((ff + 2 * deep, deep), bf16),
        ],
        [((rows, ff), f32)],
    )(pos, gate, up, cotangent, weight, basis)

    tile = lax.all_gather(hidden, "zl", axis=0, tiled=True, axis_index_groups=[ORDER])
    got = lax.all_to_all(pack, ("zl", "zh"), 0, 0, tiled=True).reshape(rows, cols)
    boths = [both, shift(both, "x", NX, 1), both, shift(both, "x", NX, 3)]
    got, *boths = lax.optimization_barrier((got, *boths))
    boths[2] = shift(boths[2], "x", NX, 2)
    cots = [got] + [shift(got, "y", NY, by) for by in range(1, NY)]
    cots = cots + [shift(piece, "c", NC, 1) for piece in cots]

    partial, reduced = call(
        backward,
        12,
        [((NZ * rows, ff), bf16), ((NZ * rows, rank), bf16)],
        [((NZ * rows, cols), bf16)],
        flops=3 * 10**9,
    )(pos, *cots, *boths)
    grad_hidden = lax.psum_scatter(
        partial, "zl", scatter_dimension=0, tiled=True, axis_index_groups=[ORDER]
    )
    (parts,) = call(
        project, 2, [((NX, NZ * slot, rank), bf16)], [((ff, rank), f32)], flops=10**9
    )(pos, tile, reduced)
    total = lax.all_to_all(parts, "x", 0, 0, tiled=True).astype(f32).sum(0)
    total, tile = lax.optimization_barrier((total.astype(bf16), tile))
    *term, leave = call(
        forward, 5, [((rows, cols), bf16)] * NY + [((NY, rows, cols), bf16)], flops=2 * 10**9
    )(pos, tile, *boths)
    arrived = shift(leave, "c", NC, 1)
    term = [(term[yr].astype(f32) + arrived[yr].astype(f32)).astype(bf16) for yr in range(NY)]
    outer = term[0].astype(f32)
    for by in range(1, NY):
        outer = outer + shift(term[by], "y", NY, -by).astype(f32)
    outer = outer.astype(bf16).reshape(NZ * NH, mine, cols)
    total = lax.all_to_all(total, "zl", 0, 0, tiled=True).reshape(NZ, slot, rank)
    projected = total.astype(f32).sum(0)[:own]
    moment1_new = 0.9 * moment1 + 0.1 * projected
    moment2_new = 0.999 * moment2 + 0.001 * projected * projected
    step = (moment1_new / corr_first / (jnp.sqrt(moment2_new / corr_second) + 1e-08)).astype(bf16)
    step = jnp.pad(step, ((0, slot - own), (0, 0)))
    step = jnp.broadcast_to(step[None], (NZ, slot, rank))
    step = lax.all_to_all(step, "zl", 0, 0, tiled=True).reshape(NZ * slot, rank)
    steps = [step] + [shift(step, "x", NX, by) for by in range(1, NX)]
    outer, steps[1] = lax.optimization_barrier((outer, steps[1]))
    (expansion,) = call(
        expand,
        5,
        [((ff, deep), f32)],
        [((NX, NZ * slot, rank), f32), ((ff, rank), f32)],
        flops=3 * 10**8,
    )(pos, *steps, basis)

    outer = lax.all_to_all(outer, ("zl", "zh"), 0, 0, tiled=True)
    (layer_out,) = call(finish_out, 1, [((mine, width), bf16)])(pos, outer)
    grad_gate, grad_up = call(
        finish_grad,
        3,
        [((rows, ff), bf16), ((rows, ff), bf16)],
        [((rows, ff), f32), ((rows, ff), f32)],
    )(pos, grad_hidden, gate, up)
    return (layer_out, grad_gate, grad_up, moment1_new, moment2_new, expansion)


def solution(mesh):
    fine = Mesh(mesh.devices.reshape(NZ, NX, NY, NH, NC), ("zl", "x", "y", "zh", "c"))
    dp, tensor = ("zl", "x"), ("y", "zh", "c")
    placed = (
        P(dp, tensor),
        P(dp, tensor),
        P(tensor, dp),
        P(dp, None),
        P(dp + tensor, None),
        P(tensor + dp, None),
        P(tensor + dp, None),
    )
    return jax.shard_map(
        body,
        mesh=fine,
        in_specs=placed,
        out_specs=(
            P(dp + tensor, None),
            P(dp, tensor),
            P(dp, tensor),
            P(tensor + dp, None),
            P(tensor + dp, None),
            P(tensor, dp),
        ),
        check_vma=False,
    )
```

```python
import jax
import jax.numpy as jnp
from jax import lax
from jax.experimental import pallas as pl
from jax.experimental.pallas import tpu as pltpu
from jax.sharding import Mesh, PartitionSpec as P

corr_first = 1.0 - 0.9**10
corr_second = 1.0 - 0.999**10

NZ, NX, NY, NH, NC = 8, 4, 4, 2, 2
ORDER = (0, 2, 4, 6, 7, 5, 3, 1)
bf16, f32 = jnp.bfloat16, jnp.float32
VMEM = pl.BlockSpec(memory_space=pltpu.VMEM)
SMEM = pl.BlockSpec(memory_space=pltpu.SMEM)


def shift(value, axis, size, by):
    return lax.ppermute(value, axis, [(i, (i - by) % size) for i in range(size)])


def dot(a, b, contract):
    return lax.dot_general(a, b, (contract, ((), ())), preferred_element_type=f32)


def call(kernel, n_in, outs, scratch=(), flops=0, limit=20):
    return pl.pallas_call(
        kernel,
        out_shape=tuple(jax.ShapeDtypeStruct(*o) for o in outs),
        in_specs=[SMEM] + [VMEM] * n_in,
        out_specs=tuple(VMEM for _ in outs),
        scratch_shapes=[pltpu.VMEM(*s) for s in scratch],
        compiler_params=pltpu.CompilerParams(vmem_limit_bytes=limit << 20),
        cost_estimate=pl.CostEstimate(flops=flops, bytes_accessed=4 << 20, transcendentals=0),
    )


def join(pos, weight, basis, both):
    both[:896, :] = weight[...]
    both[896:1152, :] = basis[:, :256]
    both[1152:, :] = basis[:, 256:]


def prepare(pos, gate, up, cot, hidden, pack, plain):
    x, y, c = pos[0], pos[1], pos[2]
    for r in range(NX):
        block = lax.rem(x + r, NX) * 256
        for zl in range(NZ):
            piece = cot[:, pl.ds(pl.multiple_of(zl * 1024 + block, 256), 256)]
            for zh in range(NH):
                pack[zl * NH + zh, :, r * 256 : (r + 1) * 256] = piece
    g = gate[...].astype(f32)
    plain[...] = g * jax.nn.sigmoid(g) * up[...].astype(f32)
    for cr in range(NC):
        for yr in range(NY):
            first = (lax.rem(y + yr, NY) * 4 + lax.rem(c + cr, NC)) * 8
            pair = [plain[pl.ds(pl.multiple_of(first + zh * 16, 8), 8), :] for zh in range(NH)]
            hidden[pl.ds((cr * NY + yr) * 16, 16), :] = jnp.concatenate(pair, 0).astype(bf16)


def reduce(pos, *refs):
    cots, boths = refs[:8], refs[8:12]
    tile, reduced = refs[12:]
    for piece in range(8):
        for at, zl in enumerate(ORDER):
            tile[pl.ds(at * 128 + piece * 16, 16), :] = cots[piece][pl.ds(zl * 16, 16), :]

    def rows(step, _):
        at = pl.ds(pl.multiple_of(step * 256, 256), 256)
        for side in range(2):
            total = None
            for r in range(NX):
                part = boths[r][896 + side * 256 : 1152 + side * 256, :]
                more = dot(tile[at, r * 256 : (r + 1) * 256], part, ((1,), (0,)))
                total = more if total is None else total + more
            reduced[at, side * 256 : (side + 1) * 256] = total.astype(bf16)
        return 0

    lax.fori_loop(0, 4, rows, 0)


def backward(pos, tile, b0, b1, b2, b3, grad):
    def rows(step, _):
        at = pl.ds(pl.multiple_of(step * 256, 256), 256)
        total = None
        for r, both in enumerate((b0, b1, b2, b3)):
            more = dot(tile[at, r * 256 : (r + 1) * 256], both[:896, :], ((1,), (1,)))
            total = more if total is None else total + more
        grad[at, :] = total.astype(bf16)
        return 0

    lax.fori_loop(0, 4, rows, 0)


def project(pos, tile, reduced, out, total):
    total[...] = dot(tile[...], reduced[...], ((0,), (0,)))
    spare = jnp.zeros((4, total.shape[1]), f32)
    for xs in range(NX):
        for zl in range(NZ):
            first = zl * 112 + xs * 28
            block = jnp.concatenate([total[first : first + 28, :], spare], 0)
            out[xs, zl * 32 : zl * 32 + 32, :] = block.astype(bf16)


def forward(pos, tile, b0, b1, b2, b3, o0, o1, o2, o3, leave):
    for step in range(4):
        part = tile[step * 256 : (step + 1) * 256, :]
        for r, both in enumerate((b0, b1, b2, b3)):
            term = dot(part, both[:896, :], ((1,), (0,))).astype(bf16)
            for half in range(2):
                zl = ORDER[step * 2 + half]
                to = pl.ds(zl * 16, 16)
                for piece in range(8):
                    first = half * 128 + piece * 16
                    block = term[first : first + 16, :]
                    if piece < NY:
                        (o0, o1, o2, o3)[piece][to, r * 256 : (r + 1) * 256] = block
                    else:
                        leave[piece - NY, to, r * 256 : (r + 1) * 256] = block


def finish_out(pos, parts, out):
    x = pos[0]
    for zl in range(NZ):
        both = (parts[zl * NH].astype(f32) + parts[zl * NH + 1].astype(f32)).astype(bf16)
        for r in range(NX):
            block = zl * 1024 + lax.rem(x + r, NX) * 256
            out[:, pl.ds(pl.multiple_of(block, 256), 256)] = both[:, r * 256 : (r + 1) * 256]


def finish_grad(pos, total, gate, up, grad_gate, grad_up, relative, plain):
    y, c = pos[1], pos[2]
    relative[...] = total[...].astype(f32)
    for ys in range(NY):
        yr = lax.rem(ys - y + NY, NY)
        for zh in range(NH):
            for cs in range(NC):
                cr = lax.rem(cs + c, NC)
                first = ((cr * NY + yr) * NH + zh) * 8
                to = ((ys * NH + zh) * NC + cs) * 8
                plain[to : to + 8, :] = relative[pl.ds(pl.multiple_of(first, 8), 8), :]
    g, u, d = gate[...].astype(f32), up[...].astype(f32), plain[...]
    s = jax.nn.sigmoid(g)
    grad_up[...] = (d * g * s).astype(bf16)
    grad_gate[...] = (d * u * s * (1.0 + g * (1.0 - s))).astype(bf16)


def expand(pos, s0, s1, s2, s3, basis, out, pieces, steps):
    x = pos[0]
    for xr, piece in enumerate((s0, s1, s2, s3)):
        pieces[lax.rem(x + xr, NX)] = piece[...].astype(f32)
    for xs in range(NX):
        for zl in range(NZ):
            first = zl * 112 + xs * 28
            steps[first : first + 28, :] = pieces[xs, zl * 32 : zl * 32 + 28, :]
    out[...] = dot(steps[...].astype(bf16), basis[...], ((1,), (1,)))


def body(gate, up, weight, basis, cotangent, moment1, moment2):
    pos = jnp.stack([lax.axis_index(a) for a in ("x", "y", "c")]).astype(jnp.int32)
    rows, ff = gate.shape
    mine, width = cotangent.shape
    cols = width // NZ
    deep, rank = basis.shape
    own, slot = moment1.shape[0], 32

    hidden, pack = call(
        prepare, 3, [((rows, ff), bf16), ((NZ * NH, mine, cols), bf16)], [((rows, ff), f32)]
    )(pos, gate, up, cotangent)
    pack, hidden, weight = lax.optimization_barrier((pack, hidden, weight))
    (both,) = call(join, 2, [((ff + 2 * deep, deep), bf16)])(pos, weight, basis)

    tile = lax.all_gather(hidden, "zl", axis=0, tiled=True, axis_index_groups=[ORDER])
    got = lax.all_to_all(pack, ("zl", "zh"), 0, 0, tiled=True).reshape(rows, cols)
    boths = [both, shift(both, "x", NX, 1), both, shift(both, "x", NX, 3)]
    got, *boths = lax.optimization_barrier((got, *boths))
    boths[2] = shift(boths[2], "x", NX, 2)
    cots = [got] + [shift(got, "y", NY, by) for by in range(1, NY)]
    cots = cots + [shift(piece, "c", NC, 1) for piece in cots]

    tile_cot, reduced = call(
        reduce,
        12,
        [((NZ * rows, cols), bf16), ((NZ * rows, rank), bf16)],
        flops=10**9,
    )(pos, *cots, *boths)

    (parts,) = call(
        project, 2, [((NX, NZ * slot, rank), bf16)], [((ff, rank), f32)], flops=10**9
    )(pos, tile, reduced)
    tile_cot, parts = lax.optimization_barrier((tile_cot, parts))
    (partial,) = call(backward, 5, [((NZ * rows, ff), bf16)], flops=2 * 10**9)(
        pos, tile_cot, *boths
    )
    grad_hidden = lax.psum_scatter(
        partial, "zl", scatter_dimension=0, tiled=True, axis_index_groups=[ORDER]
    )
    total = lax.all_to_all(parts, "x", 0, 0, tiled=True).astype(f32).sum(0)
    total, tile, partial = lax.optimization_barrier((total.astype(bf16), tile, partial))
    *term, leave = call(
        forward, 5, [((rows, cols), bf16)] * NY + [((NY, rows, cols), bf16)], flops=2 * 10**9
    )(pos, tile, *boths)
    arrived = shift(leave, "c", NC, 1)
    term = [(term[yr].astype(f32) + arrived[yr].astype(f32)).astype(bf16) for yr in range(NY)]
    total = lax.all_to_all(total, "zl", 0, 0, tiled=True).reshape(NZ, slot, rank)
    projected = total.astype(f32).sum(0)[:own]
    moment1_new = 0.9 * moment1 + 0.1 * projected
    moment2_new = 0.999 * moment2 + 0.001 * projected * projected
    step = (moment1_new / corr_first / (jnp.sqrt(moment2_new / corr_second) + 1e-08)).astype(bf16)
    step = jnp.pad(step, ((0, slot - own), (0, 0)))
    step, *term = lax.optimization_barrier((step, *term))
    step = jnp.broadcast_to(step[None], (NZ, slot, rank))
    step = lax.all_to_all(step, "zl", 0, 0, tiled=True).reshape(NZ * slot, rank)
    outer = term[0].astype(f32)
    for by in range(1, NY):
        outer = outer + shift(term[by], "y", NY, -by).astype(f32)
    outer = outer.astype(bf16).reshape(NZ * NH, mine, cols)
    step, outer = lax.optimization_barrier((step, outer))
    steps = [step] + [shift(step, "x", NX, by) for by in range(1, NX)]
    (expansion,) = call(
        expand,
        5,
        [((ff, deep), f32)],
        [((NX, NZ * slot, rank), f32), ((ff, rank), f32)],
        flops=3 * 10**8,
    )(pos, *steps, basis)

    outer = lax.all_to_all(outer, ("zl", "zh"), 0, 0, tiled=True)
    (layer_out,) = call(finish_out, 1, [((mine, width), bf16)])(pos, outer)
    grad_gate, grad_up = call(
        finish_grad,
        3,
        [((rows, ff), bf16), ((rows, ff), bf16)],
        [((rows, ff), f32), ((rows, ff), f32)],
    )(pos, grad_hidden, gate, up)
    return (layer_out, grad_gate, grad_up, moment1_new, moment2_new, expansion)


def solution(mesh):
    fine = Mesh(mesh.devices.reshape(NZ, NX, NY, NH, NC), ("zl", "x", "y", "zh", "c"))
    dp, tensor = ("zl", "x"), ("y", "zh", "c")
    placed = (
        P(dp, tensor),
        P(dp, tensor),
        P(tensor, dp),
        P(dp, None),
        P(dp + tensor, None),
        P(tensor + dp, None),
        P(tensor + dp, None),
    )
    return jax.shard_map(
        body,
        mesh=fine,
        in_specs=placed,
        out_specs=(
            P(dp + tensor, None),
            P(dp, tensor),
            P(dp, tensor),
            P(tensor + dp, None),
            P(tensor + dp, None),
            P(tensor, dp),
        ),
        check_vma=False,
    )
```

```python
import jax
import jax.numpy as jnp
from jax import lax
from jax.experimental import pallas as pl
from jax.experimental.pallas import tpu as pltpu
from jax.sharding import Mesh, PartitionSpec as P

corr_first = 1.0 - 0.9**10
corr_second = 1.0 - 0.999**10

NZ, NX, NY, NH, NC = 8, 4, 4, 2, 2
ORDER = (0, 2, 4, 6, 7, 5, 3, 1)
bf16, f32 = jnp.bfloat16, jnp.float32
VMEM = pl.BlockSpec(memory_space=pltpu.VMEM)
SMEM = pl.BlockSpec(memory_space=pltpu.SMEM)


def shift(value, axis, size, by):
    return lax.ppermute(value, axis, [(i, (i - by) % size) for i in range(size)])


def dot(a, b, contract):
    return lax.dot_general(a, b, (contract, ((), ())), preferred_element_type=f32)


def call(kernel, n_in, outs, scratch=(), flops=0, limit=20):
    return pl.pallas_call(
        kernel,
        out_shape=tuple(jax.ShapeDtypeStruct(*o) for o in outs),
        in_specs=[SMEM] + [VMEM] * n_in,
        out_specs=tuple(VMEM for _ in outs),
        scratch_shapes=[pltpu.VMEM(*s) for s in scratch],
        compiler_params=pltpu.CompilerParams(vmem_limit_bytes=limit << 20),
        cost_estimate=pl.CostEstimate(flops=flops, bytes_accessed=4 << 20, transcendentals=0),
    )


def join(pos, weight, basis, both):
    both[:896, :] = weight[...]
    both[896:1152, :] = basis[:, :256]
    both[1152:, :] = basis[:, 256:]


def prepare(pos, gate, up, cot, hidden, pack, plain):
    x, y, c = pos[0], pos[1], pos[2]
    for r in range(NX):
        block = lax.rem(x + r, NX) * 256
        for zl in range(NZ):
            piece = cot[:, pl.ds(pl.multiple_of(zl * 1024 + block, 256), 256)]
            for zh in range(NH):
                pack[zl * NH + zh, :, r * 256 : (r + 1) * 256] = piece
    g = gate[...].astype(f32)
    plain[...] = g * jax.nn.sigmoid(g) * up[...].astype(f32)
    for cr in range(NC):
        for yr in range(NY):
            first = (lax.rem(y + yr, NY) * 4 + lax.rem(c + cr, NC)) * 8
            pair = [plain[pl.ds(pl.multiple_of(first + zh * 16, 8), 8), :] for zh in range(NH)]
            hidden[pl.ds((cr * NY + yr) * 16, 16), :] = jnp.concatenate(pair, 0).astype(bf16)


def reduce(pos, *refs):
    cots, boths = refs[:8], refs[8:12]
    tile, reduced = refs[12:]
    for piece in range(8):
        for at, zl in enumerate(ORDER):
            tile[pl.ds(at * 128 + piece * 16, 16), :] = cots[piece][pl.ds(zl * 16, 16), :]

    def rows(step, _):
        at = pl.ds(pl.multiple_of(step * 256, 256), 256)
        for side in range(2):
            total = None
            for r in range(NX):
                part = boths[r][896 + side * 256 : 1152 + side * 256, :]
                more = dot(tile[at, r * 256 : (r + 1) * 256], part, ((1,), (0,)))
                total = more if total is None else total + more
            reduced[at, side * 256 : (side + 1) * 256] = total.astype(bf16)
        return 0

    lax.fori_loop(0, 4, rows, 0)


def backward(pos, tile, b0, b1, b2, b3, grad):
    def rows(step, _):
        at = pl.ds(pl.multiple_of(step * 256, 256), 256)
        total = None
        for r, both in enumerate((b0, b1, b2, b3)):
            more = dot(tile[at, r * 256 : (r + 1) * 256], both[:896, :], ((1,), (1,)))
            total = more if total is None else total + more
        grad[at, :] = total.astype(bf16)
        return 0

    lax.fori_loop(0, 4, rows, 0)


def project(pos, tile, reduced, out, total):
    total[...] = dot(tile[...], reduced[...], ((0,), (0,)))
    spare = jnp.zeros((4, total.shape[1]), f32)
    for xs in range(NX):
        for zl in range(NZ):
            first = zl * 112 + xs * 28
            block = jnp.concatenate([total[first : first + 28, :], spare], 0)
            out[xs, zl * 32 : zl * 32 + 32, :] = block.astype(bf16)


def forward(pos, tile, b0, b1, b2, b3, o0, o1, o2, o3, leave):
    for step in range(4):
        part = tile[step * 256 : (step + 1) * 256, :]
        for r, both in enumerate((b0, b1, b2, b3)):
            term = dot(part, both[:896, :], ((1,), (0,))).astype(bf16)
            for half in range(2):
                zl = ORDER[step * 2 + half]
                to = pl.ds(zl * 16, 16)
                for piece in range(8):
                    first = half * 128 + piece * 16
                    block = term[first : first + 16, :]
                    if piece < NY:
                        (o0, o1, o2, o3)[piece][to, r * 256 : (r + 1) * 256] = block
                    else:
                        leave[piece - NY, to, r * 256 : (r + 1) * 256] = block


def finish_out(pos, parts, out):
    x = pos[0]
    for zl in range(NZ):
        both = (parts[zl * NH].astype(f32) + parts[zl * NH + 1].astype(f32)).astype(bf16)
        for r in range(NX):
            block = zl * 1024 + lax.rem(x + r, NX) * 256
            out[:, pl.ds(pl.multiple_of(block, 256), 256)] = both[:, r * 256 : (r + 1) * 256]


def finish_grad(pos, total, gate, up, grad_gate, grad_up, relative, plain):
    y, c = pos[1], pos[2]
    relative[...] = total[...].astype(f32)
    for ys in range(NY):
        yr = lax.rem(ys - y + NY, NY)
        for zh in range(NH):
            for cs in range(NC):
                cr = lax.rem(cs + c, NC)
                first = ((cr * NY + yr) * NH + zh) * 8
                to = ((ys * NH + zh) * NC + cs) * 8
                plain[to : to + 8, :] = relative[pl.ds(pl.multiple_of(first, 8), 8), :]
    g, u, d = gate[...].astype(f32), up[...].astype(f32), plain[...]
    s = jax.nn.sigmoid(g)
    grad_up[...] = (d * g * s).astype(bf16)
    grad_gate[...] = (d * u * s * (1.0 + g * (1.0 - s))).astype(bf16)


def expand(pos, s0, s1, s2, s3, basis, out, pieces, steps):
    x = pos[0]
    for xr, piece in enumerate((s0, s1, s2, s3)):
        pieces[lax.rem(x + xr, NX)] = piece[...].astype(f32)
    for xs in range(NX):
        for zl in range(NZ):
            first = zl * 112 + xs * 28
            steps[first : first + 28, :] = pieces[xs, zl * 32 : zl * 32 + 28, :]
    out[...] = dot(steps[...].astype(bf16), basis[...], ((1,), (1,)))


def body(gate, up, weight, basis, cotangent, moment1, moment2):
    pos = jnp.stack([lax.axis_index(a) for a in ("x", "y", "c")]).astype(jnp.int32)
    rows, ff = gate.shape
    mine, width = cotangent.shape
    cols = width // NZ
    deep, rank = basis.shape
    own, slot = moment1.shape[0], 32

    hidden, pack = call(
        prepare, 3, [((rows, ff), bf16), ((NZ * NH, mine, cols), bf16)], [((rows, ff), f32)]
    )(pos, gate, up, cotangent)
    pack, hidden, weight = lax.optimization_barrier((pack, hidden, weight))
    (both,) = call(join, 2, [((ff + 2 * deep, deep), bf16)])(pos, weight, basis)

    tile = lax.all_gather(hidden, "zl", axis=0, tiled=True, axis_index_groups=[ORDER])
    got = lax.all_to_all(pack, ("zl", "zh"), 0, 0, tiled=True).reshape(rows, cols)
    boths = [both, shift(both, "x", NX, 1), both, shift(both, "x", NX, 3)]
    got, *boths = lax.optimization_barrier((got, *boths))
    boths[2] = shift(boths[2], "x", NX, 2)
    cots = [got] + [shift(got, "y", NY, by) for by in range(1, NY)]
    cots = cots + [shift(piece, "c", NC, 1) for piece in cots]

    tile_cot, reduced = call(
        reduce,
        12,
        [((NZ * rows, cols), bf16), ((NZ * rows, rank), bf16)],
        flops=10**9,
    )(pos, *cots, *boths)

    (parts,) = call(
        project, 2, [((NX, NZ * slot, rank), bf16)], [((ff, rank), f32)], flops=10**9
    )(pos, tile, reduced)
    tile_cot, parts = lax.optimization_barrier((tile_cot, parts))
    (partial,) = call(backward, 5, [((NZ * rows, ff), bf16)], flops=2 * 10**9)(
        pos, tile_cot, *boths
    )
    grad_hidden = lax.psum_scatter(
        partial, "zl", scatter_dimension=0, tiled=True, axis_index_groups=[ORDER]
    )
    total = lax.all_to_all(parts, "x", 0, 0, tiled=True).astype(f32).sum(0)
    total, tile, partial = lax.optimization_barrier((total.astype(bf16), tile, partial))
    *term, leave = call(
        forward, 5, [((rows, cols), bf16)] * NY + [((NY, rows, cols), bf16)], flops=2 * 10**9
    )(pos, tile, *boths)
    arrived = shift(leave, "c", NC, 1)
    term = [(term[yr].astype(f32) + arrived[yr].astype(f32)).astype(bf16) for yr in range(NY)]
    total = lax.all_to_all(total, "zl", 0, 0, tiled=True).reshape(NZ, slot, rank)
    projected = total.astype(f32).sum(0)[:own]
    moment1_new = 0.9 * moment1 + 0.1 * projected
    moment2_new = 0.999 * moment2 + 0.001 * projected * projected
    step = (moment1_new / corr_first / (jnp.sqrt(moment2_new / corr_second) + 1e-08)).astype(bf16)
    step = jnp.pad(step, ((0, slot - own), (0, 0)))
    step, *term = lax.optimization_barrier((step, *term))
    step = jnp.broadcast_to(step[None], (NZ, slot, rank))
    step = lax.all_to_all(step, "zl", 0, 0, tiled=True).reshape(NZ * slot, rank)
    outer = term[0].astype(f32)
    for by in range(1, NY):
        outer = outer + shift(term[by], "y", NY, -by).astype(f32)
    outer = outer.astype(bf16).reshape(NZ * NH, mine, cols)
    step, outer = lax.optimization_barrier((step, outer))
    steps = [step] + [shift(step, "x", NX, by) for by in range(1, NX)]
    steps[1], grad_hidden = lax.optimization_barrier((steps[1], grad_hidden))
    (expansion,) = call(
        expand,
        5,
        [((ff, deep), f32)],
        [((NX, NZ * slot, rank), f32), ((ff, rank), f32)],
        flops=3 * 10**8,
    )(pos, *steps, basis)

    outer = lax.all_to_all(outer, ("zl", "zh"), 0, 0, tiled=True)
    (layer_out,) = call(finish_out, 1, [((mine, width), bf16)])(pos, outer)
    grad_gate, grad_up = call(
        finish_grad,
        3,
        [((rows, ff), bf16), ((rows, ff), bf16)],
        [((rows, ff), f32), ((rows, ff), f32)],
    )(pos, grad_hidden, gate, up)
    return (layer_out, grad_gate, grad_up, moment1_new, moment2_new, expansion)


def solution(mesh):
    fine = Mesh(mesh.devices.reshape(NZ, NX, NY, NH, NC), ("zl", "x", "y", "zh", "c"))
    dp, tensor = ("zl", "x"), ("y", "zh", "c")
    placed = (
        P(dp, tensor),
        P(dp, tensor),
        P(tensor, dp),
        P(dp, None),
        P(dp + tensor, None),
        P(tensor + dp, None),
        P(tensor + dp, None),
    )
    return jax.shard_map(
        body,
        mesh=fine,
        in_specs=placed,
        out_specs=(
            P(dp + tensor, None),
            P(dp, tensor),
            P(dp, tensor),
            P(tensor + dp, None),
            P(tensor + dp, None),
            P(tensor, dp),
        ),
        check_vma=False,
    )
```
